256 devices in a mesh: sector: 64 (over x, y_hi, z), slab: 4 (over y_lo, core).
Axes of the slice: x: 4, y: 4 (y_hi: 2, y_lo: 2; y = y_hi * 2 + y_lo), z: 8, core: 2. Of those that a mesh axis runs over, the one named last changes fastest.
Arguments:
- measured: float32 [64, 262144], P('slab', 'sector'), may hold values from -64 to 64
- tof: bfloat16 [512, 16, 2, 128, 128], P('sector'), may hold values from -0.1875 to 0.1875
- tof_rows: int32 [512, 16, 2], P('sector'), may hold values from 0 to 31
- tile_owner: int32 [64], replicated, may hold values from 0 to 63, each once
Outputs:
- image: float32 [64, 131072], P('slab', 'sector')
- data_dual: float32 [64, 262144], P('slab', 'sector')
- wavelet_dual: float32 [64, 131072], P('slab', 'sector')
The draws below stay inside these ranges and needn't reach their ends.
Inputs may be any that keep to these rules, and one draw needn't show every extreme that they name: `tile_owner`: each tile 0 to 63 is named exactly once.
All inputs are finite; a program needn't handle non-finite values.
Results may differ from the reference program's by a relative error of at most 0.0035.
Values may be sent and summed in bfloat16 or wider, within the bound.
A program may use at most 128 MiB of HBM per device.

```python
import jax
import jax.numpy as jnp
from jax import lax

BLK = 128
STOPS = 8
SLOTS = 2
NBD = 16
TB = 32
ITERS = 3
SECTORS = 64
DEPTH = 64
PW = 32
NPIX = 131072
NDATA = 262144


def place_ends(result, own_key, smallest, top_value):
    dims = result.shape
    place = [jax.random.randint(jax.random.fold_in(own_key, axis), (), 0, dims[axis]) for axis in range(len(dims))]
    result = result.at[tuple(place)].set(smallest)
    longest = dims.index(max(dims))
    place[longest] = (place[longest] + 1) % dims[longest]
    return result.at[tuple(place)].set(top_value)


def steps_of(stream_key, dims, cuts, least, high):
    def one(axis_at, parts):
        heights = jax.random.uniform(jax.random.fold_in(jax.random.fold_in(stream_key, 6), axis_at), (parts,), jnp.float32, least / len(cuts), high / len(cuts))
        return jnp.repeat(jnp.exp(heights), dims[axis_at] // parts).reshape((-1,) + (1,) * (len(dims) - axis_at - 1))

    gain = one(*cuts[0])
    for cut in cuts[1:]:
        gain = gain * one(*cut)
    return gain


def noise(rng, dims, deviation, bound, split=(), held_as=jnp.bfloat16):
    array = deviation * jax.random.normal(rng, dims, jnp.float32)
    if split:
        array = array * steps_of(rng, dims, split, -0.22, 0.18)
    return jnp.clip(array, -bound, bound).astype(held_as)


def setup_inputs(seed: int = 0) -> dict:
    arg_keys = jax.random.split(jax.random.key(seed), 5)
    measured = noise(arg_keys[0], (DEPTH, NDATA), 10.0, 64.0, ((0, 4), (1, 64)), jnp.float32)
    tof = noise(arg_keys[1], (SECTORS * STOPS, NBD, SLOTS, BLK, BLK), (BLK * STOPS * NBD * SLOTS // TB) ** -0.5, 0.1875, ((0, 64),))
    tof_rows = place_ends(jax.random.randint(arg_keys[2], (SECTORS * STOPS, NBD, SLOTS), 0, TB), jax.random.fold_in(arg_keys[2], 1), 0, TB - 1).astype(jnp.int32)
    tile_owner = jax.random.permutation(arg_keys[3], SECTORS).astype(jnp.int32)
    return dict(measured=measured, tof=tof, tof_rows=tof_rows, tile_owner=tile_owner)


dual_step = 0.5
primal_step = 0.15
wave_limit = 0.5
depth_limit = 0.5


def haar_pairs(upper_row, lower_row):
    sum_up = upper_row[..., 0] + upper_row[..., 1]
    dif_up = upper_row[..., 0] - upper_row[..., 1]
    sum_low = lower_row[..., 0] + lower_row[..., 1]
    dif_low = lower_row[..., 0] - lower_row[..., 1]
    top_row = jnp.stack([(sum_up + sum_low) * 0.5, (dif_up + dif_low) * 0.5], -1)
    low_row = jnp.stack([(sum_up - sum_low) * 0.5, (dif_up - dif_low) * 0.5], -1)
    return top_row, low_row


def haar_tiles(tiles):
    shaped = tiles.reshape(DEPTH, SECTORS, SECTORS // 2, 2, PW // 2, 2)
    top_row, low_row = haar_pairs(shaped[:, :, :, 0], shaped[:, :, :, 1])
    return jnp.stack([top_row, low_row], 3).reshape(DEPTH, NPIX)


def to_tiles(field, tile_owner):
    inverse = jnp.argsort(tile_owner)
    shaped = field.reshape(DEPTH, SECTORS, SECTORS, PW)[:, :, inverse, :]
    return shaped.transpose(0, 2, 1, 3).reshape(DEPTH, NPIX)


def from_tiles(tiles, tile_owner):
    shaped = tiles.reshape(DEPTH, SECTORS, SECTORS, PW)[:, tile_owner, :, :]
    return shaped.transpose(0, 2, 1, 3).reshape(DEPTH, NPIX)


def depth_diff(field):
    return jnp.concatenate([field[1:] - field[:-1], jnp.zeros_like(field[:1])], 0)


def depth_back(dual):
    return jnp.concatenate([jnp.zeros_like(dual[:1]), dual[:-1]], 0) - dual


def reference(measured, tof, tof_rows, tile_owner):
    blocks_all = tof.reshape(SECTORS, STOPS, NBD, SLOTS, BLK, BLK)
    rows_all = tof_rows.reshape(SECTORS, STOPS, NBD, SLOTS)
    stop_ids = jnp.arange(STOPS, dtype=jnp.int32)

    def forward(image_half):
        shares = image_half.astype(jnp.float32).reshape(DEPTH, SECTORS, NBD, BLK)

        def one_sector(sector):
            owners = (sector + stop_ids - STOPS // 2) % SECTORS
            pieces = shares[:, owners]
            mats = blocks_all[sector].astype(jnp.float32)
            terms = jnp.einsum("djbp,jbkrp->jbkdr", pieces, mats).reshape(STOPS * NBD * SLOTS, DEPTH, BLK)
            return jax.ops.segment_sum(terms, rows_all[sector].reshape(-1), num_segments=TB)

        sums = lax.map(one_sector, jnp.arange(SECTORS, dtype=jnp.int32))
        return sums.transpose(2, 0, 1, 3).reshape(DEPTH, NDATA)

    def adjoint(dual_half):
        duals = dual_half.astype(jnp.float32).reshape(DEPTH, SECTORS, TB, BLK)

        def add_sector(sector, total):
            sector = sector.astype(jnp.int32)
            picked = duals[:, sector][:, rows_all[sector]]
            mats = blocks_all[sector].astype(jnp.float32)
            gathered = jnp.einsum("djbkr,jbkrp->jbdp", picked, mats)
            owners = (sector + stop_ids - STOPS // 2) % SECTORS
            return total.at[owners].add(gathered)

        total = lax.fori_loop(0, SECTORS, add_sector, jnp.zeros((SECTORS, NBD, DEPTH, BLK), jnp.float32))
        return total.transpose(2, 0, 1, 3).reshape(DEPTH, NPIX)

    image = jnp.zeros((DEPTH, NPIX), jnp.float32)
    xbar = jnp.zeros((DEPTH, NPIX), jnp.float32)
    depth_dual = jnp.zeros((DEPTH, NPIX), jnp.float32)
    wavelet_dual = jnp.zeros((DEPTH, NPIX), jnp.float32)
    data_dual = jnp.zeros((DEPTH, NDATA), jnp.float32)
    for iteration in range(ITERS):
        forward_data = forward(xbar.astype(jnp.bfloat16))
        data_dual = (data_dual + dual_step * (forward_data - measured)) / (1.0 + dual_step)
        wavelet_dual = jnp.clip(wavelet_dual + dual_step * haar_tiles(to_tiles(xbar, tile_owner)), -wave_limit, wave_limit)
        depth_dual = jnp.clip(depth_dual + dual_step * depth_diff(xbar), -depth_limit, depth_limit)
        back = adjoint(data_dual.astype(jnp.bfloat16))
        wave_back = from_tiles(haar_tiles(wavelet_dual), tile_owner)
        update = back + wave_back + depth_back(depth_dual)
        image_new = jnp.maximum(image - primal_step * update, 0.0)
        xbar = 2.0 * image_new - image
        image = image_new
    return image, data_dual, wavelet_dual
```

```python
import functools

import jax
import jax.numpy as jnp
from jax import lax
from jax.experimental import pallas as pl
from jax.experimental.pallas import tpu as pltpu
from jax.sharding import PartitionSpec as P

ITERS = 3
STOPS = 8
HALF = STOPS // 2
ZS = 8

dual_step = 0.5
primal_step = 0.15
wave_limit = 0.5
depth_limit = 0.5


def far_first(i):
    return (i % 2) * (STOPS - 1) + (1 - 2 * (i % 2)) * (i // 2)


def near_first(i):
    return far_first(6 - i)


def kernel(
    sectors, groups, slabs, blocks, time_blocks,
    rows_ref, prev_ref, owner_ref, inverse_ref, measured_ref, tof_hbm,
    image_ref, data_ref, wave_ref,
    tof, sums, dual_half, xbar, depth, halo, total,
    shares, partials_out, partials_in, edge_out, edge_in,
    rolled, bands, mid, tiles, wave, rolled_back, back_bands, wave_back,
    load_sem, share_send, share_recv, part_send, part_recv, edge_send, edge_recv,
    band_send, band_recv,
):
    me = lax.axis_index("sector")
    slab = lax.axis_index("slab")
    group, zed = me // ZS, lax.rem(me, ZS)
    terms = STOPS * blocks * 2

    loads = [
        pltpu.make_async_copy(tof_hbm.at[j], tof.at[j], load_sem.at[j]) for j in range(STOPS)
    ]
    for i in (0, 7, 1, 6, 2, 5, 3, 4):
        loads[i].start()

    def sector_at(offset):
        return lax.rem(me + offset + sectors, sectors)

    def group_at(offset):
        return lax.rem(group + offset, groups)

    def zed_at(offset):
        return lax.rem(zed + offset, ZS)

    def slab_at(offset):
        return lax.rem(slab + offset + slabs, slabs)

    barrier = pltpu.get_barrier_semaphore()
    greeted = 0
    for offset in range(1, HALF + 1):
        for sign in (1, -1):
            pl.semaphore_signal(barrier, inc=1, device_id={"sector": sector_at(sign * offset)})
            greeted += 1
    for offset in range(1, ZS):
        pl.semaphore_signal(barrier, inc=1, device_id={"sector": group * ZS + zed_at(offset)})
        greeted += 1
    for offset in range(1, groups):
        pl.semaphore_signal(barrier, inc=1, device_id={"sector": group_at(offset) * ZS + zed})
        greeted += 1
    for sign in (1, -1):
        pl.semaphore_signal(barrier, inc=1, device_id={"slab": slab_at(sign)})
        greeted += 1

    lanes = lax.broadcasted_iota(jnp.int32, (4, 128), 1)
    quarter = lanes // 32
    odd_lane = lax.rem(lax.broadcasted_iota(jnp.int32, (ZS, 4, 128), 2), 2) == 1
    row_ids = lax.broadcasted_iota(jnp.int32, (16, 128), 0)
    last_slab = slab == slabs - 1
    first_slab = slab == 0

    def share_copy(it, j):
        return pltpu.make_async_remote_copy(
            src_ref=shares.at[it, HALF], dst_ref=shares.at[it, j],
            send_sem=share_send.at[it, j], recv_sem=share_recv.at[it, j],
            device_id={"sector": sector_at(HALF - j)},
        )

    def part_copy(it, j):
        return pltpu.make_async_remote_copy(
            src_ref=partials_out.at[it, j], dst_ref=partials_in.at[it, j],
            send_sem=part_send.at[it, j], recv_sem=part_recv.at[it, j],
            device_id={"sector": sector_at(j - HALF)},
        )

    def edge_copy(it, way):
        return pltpu.make_async_remote_copy(
            src_ref=edge_out.at[it, way], dst_ref=edge_in.at[it, way],
            send_sem=edge_send.at[it, way], recv_sem=edge_recv.at[it, way],
            device_id={"slab": slab_at(1 if way else -1)},
        )

    def zed_copy(it, way, source, offset):
        return pltpu.make_async_remote_copy(
            src_ref=source.at[it, :, zed_at(offset)], dst_ref=mid.at[it, way, :, zed],
            send_sem=band_send.at[it, way, 0, offset], recv_sem=band_recv.at[it, way, 0, offset],
            device_id={"sector": group * ZS + zed_at(offset)},
        )

    def zed_wait(it, way, source, offset):
        pltpu.make_async_remote_copy(
            src_ref=source.at[it, :, zed_at(offset)], dst_ref=mid.at[it, way, :, zed_at(ZS - offset)],
            send_sem=band_send.at[it, way, 0, offset], recv_sem=band_recv.at[it, way, 0, offset],
            device_id={"sector": group * ZS + zed_at(offset)},
        ).wait_recv()

    def group_copy(it, way, dest, offset):
        return pltpu.make_async_remote_copy(
            src_ref=mid.at[it, way, group_at(offset)], dst_ref=dest.at[it, group],
            send_sem=band_send.at[it, way, 1, offset], recv_sem=band_recv.at[it, way, 1, offset],
            device_id={"sector": group_at(offset) * ZS + zed},
        )

    def group_wait(it, way, dest, offset):
        pltpu.make_async_remote_copy(
            src_ref=mid.at[it, way, group_at(offset)], dst_ref=dest.at[it, group_at(groups - offset)],
            send_sem=band_send.at[it, way, 1, offset], recv_sem=band_recv.at[it, way, 1, offset],
            device_id={"sector": group_at(offset) * ZS + zed},
        ).wait_recv()

    def first_hop(it, way, source):
        for offset in range(1, ZS):
            zed_copy(it, way, source, offset).start()
        mid[it, way, :, pl.ds(zed, 1)] = source[it, :, pl.ds(zed, 1)]

    def second_hop(it, way, source, dest):
        for offset in range(1, ZS):
            zed_wait(it, way, source, offset)
        for offset in range(1, groups):
            group_copy(it, way, dest, offset).start()
        dest[it, pl.ds(group, 1)] = mid[it, way, pl.ds(group, 1)]

    def finish_hops(it, way, dest):
        for offset in range(1, groups):
            group_wait(it, way, dest, offset)

    def forward_stop(it, j, step):
        for b in range(blocks):
            out = lax.dot_general(
                shares[it, j, b], tof[j, b], (((1,), (1,)), ((), ())),
                preferred_element_type=jnp.float32,
            )
            n = step * (2 * blocks) + 2 * b
            sums[n] = out[:, :128] + sums[prev_ref[n]]
            sums[n + 1] = out[:, 128:] + sums[prev_ref[n + 1]]

    def adjoint_block(j, b):
        n = j * (2 * blocks) + 2 * b
        picked = jnp.concatenate([dual_half[rows_ref[n]], dual_half[rows_ref[n + 1]]], 1)
        return jnp.dot(picked, tof[j, b], preferred_element_type=jnp.float32)

    sums[terms] = jnp.zeros((16, 128), jnp.float32)

    for t in range(time_blocks):
        span = slice(t * 128, (t + 1) * 128)
        dual = (dual_step * (0.0 - measured_ref[:, span])) / (1.0 + dual_step)
        data_ref[:, span] = dual
        dual_half[t] = dual.astype(jnp.bfloat16)

    pl.semaphore_wait(barrier, greeted)

    def adjoint_sends(it, first):
        def send_stop(i, carry):
            j = far_first(i)
            if first:
                pltpu.make_async_copy(tof_hbm.at[j], tof.at[j], load_sem.at[j]).wait()
            for b in range(blocks):
                partials_out[it, j, b] = adjoint_block(j, b).astype(jnp.bfloat16)
            part_copy(it, j).start()
            return carry

        lax.fori_loop(0, STOPS - 1, send_stop, 0)
        if first:
            loads[HALF].wait()
        for b in range(blocks):
            total[b] = adjoint_block(HALF, b)

    def adjoint_gather(it):
        def add_stop(i, carry):
            j = near_first(i)
            part_copy(it, j).wait_recv()
            for b in range(blocks):
                total[b] = total[b] + partials_in[it, j, b].astype(jnp.float32)
            return carry

        lax.fori_loop(0, STOPS - 1, add_stop, 0)

    def publish(it):
        for b in range(blocks):
            shares[it, HALF, b] = xbar[b].astype(jnp.bfloat16)

        def send(i, carry):
            share_copy(it, far_first(i)).start()
            return carry

        lax.fori_loop(0, STOPS - 1, send, 0)
        for b in range(blocks):
            edge_out[it, 0, pl.ds(b, 1)] = xbar[b, 0:1]
            edge_out[it, 1, pl.ds(b, 1)] = xbar[b, 15:16]
        edge_copy(it, 0).start()
        edge_copy(it, 1).start()
        for b in range(blocks):
            value = xbar[b]
            rolled[b] = value
            for a in range(1, 4):
                rolled[a * blocks + b] = pltpu.roll(value, 32 * a, 1)

        def gather_band(k, carry):
            j = inverse_ref[k]
            block, lane = j // 4, lax.rem(j, 4)
            parts = [
                rolled[lax.rem(r - lane + 4, 4) * blocks + block, 4 * r : 4 * r + 4]
                for r in range(4)
            ]
            low = jnp.where(quarter == 0, parts[0], parts[1])
            high = jnp.where(quarter == 2, parts[2], parts[3])
            bands[it, k // ZS, lax.rem(k, ZS)] = jnp.where(quarter < 2, low, high)
            return carry

        lax.fori_loop(0, sectors, gather_band, 0, unroll=8)
        first_hop(it, 0, bands)

    def haar(upper, lower):
        def pairs(value):
            right = pltpu.roll(value, 127, 2)
            left = pltpu.roll(value, 1, 2)
            return jnp.where(odd_lane, left - value, value + right)

        top, low = pairs(upper), pairs(lower)
        return (top + low) * 0.5, (top - low) * 0.5

    def update_wave(it):
        for g in range(groups):
            full = tiles[it, g]
            upper = jnp.concatenate([full[2 * (i // 2)][None] for i in range(ZS)], 0)
            lower = jnp.concatenate([full[2 * (i // 2) + 1][None] for i in range(ZS)], 0)
            odd = lax.rem(lax.broadcasted_iota(jnp.int32, (ZS, 4, 128), 0), 2) == 1
            top, low = haar(upper, lower)
            coeffs = jnp.where(odd, low, top)
            kept = wave[g] + dual_step * coeffs
            dual = jnp.clip(kept, -wave_limit, wave_limit)
            wave[g] = dual
            upper = jnp.concatenate([dual[2 * (i // 2)][None] for i in range(ZS)], 0)
            lower = jnp.concatenate([dual[2 * (i // 2) + 1][None] for i in range(ZS)], 0)
            top, low = haar(upper, lower)
            back_bands[it, g] = jnp.where(odd, low, top)

    def update_depth(it):
        edge_copy(it, 0).wait_recv()
        edge_copy(it, 1).wait_recv()
        following = edge_in[it, 0]
        previous = edge_in[it, 1]
        for b in range(blocks):
            value = xbar[b]
            up = jnp.where(row_ids == 15, following[b : b + 1], pltpu.roll(value, 15, 0))
            diff = up - value
            diff = jnp.where(jnp.logical_and(last_slab, row_ids == 15), 0.0, diff)
            depth[b] = jnp.clip(depth[b] + dual_step * diff, -depth_limit, depth_limit)
        edge = halo[...] + dual_step * (edge_out[it, 0] - previous)
        edge = jnp.clip(edge, -depth_limit, depth_limit)
        halo[...] = jnp.where(first_slab, 0.0, edge)

    def spread_bands(source, count):
        for g in range(count // ZS):
            value = source(g)
            rolled_back[0, pl.ds(g * ZS, ZS)] = value
            for a in range(1, 4):
                rolled_back[a, pl.ds(g * ZS, ZS)] = pltpu.roll(value, 32 * a, 2)

    def joined_bands(index, b):
        places = [index(4 * b + q) for q in range(4)]
        out = []
        for r in range(4):
            parts = [rolled_back[(q - r) % 4, places[q]] for q in range(4)]
            low = jnp.where(quarter == 0, parts[0], parts[1])
            high = jnp.where(quarter == 2, parts[2], parts[3])
            out.append(jnp.where(quarter < 2, low, high))
        return out

    adjoint_sends(0, True)
    adjoint_gather(0)
    for b in range(blocks):
        image = jnp.maximum(0.0 - primal_step * total[b], 0.0)
        image_ref[:, b * 128 : (b + 1) * 128] = image
        xbar[b] = 2.0 * image
        depth[b] = jnp.zeros((16, 128), jnp.float32)
    halo[...] = jnp.zeros_like(halo)
    wave[...] = jnp.zeros_like(wave)

    def iteration(it, carry):
        publish(it)
        forward_stop(it, HALF, 0)

        def early(i, carry):
            j = near_first(i)
            share_copy(it, j).wait_recv()
            forward_stop(it, j, i + 1)
            return carry

        lax.fori_loop(0, 3, early, 0)
        second_hop(it, 0, bands, tiles)
        lax.fori_loop(3, STOPS - 1, early, 0)
        for t in range(time_blocks):
            span = slice(t * 128, (t + 1) * 128)
            moved = sums[prev_ref[terms + t]] - measured_ref[:, span]
            dual = (data_ref[:, span] + dual_step * moved) / (1.0 + dual_step)
            data_ref[:, span] = dual
            dual_half[t] = dual.astype(jnp.bfloat16)
        adjoint_sends(it + 1, False)
        finish_hops(it, 0, tiles)
        update_wave(it)
        first_hop(it, 1, back_bands)
        update_depth(it)
        second_hop(it, 1, back_bands, wave_back)
        adjoint_gather(it + 1)
        finish_hops(it, 1, wave_back)
        spread_bands(lambda g: wave_back[it, g], sectors)
        for b in range(blocks):
            for r, part in enumerate(joined_bands(lambda j: owner_ref[j], b)):
                total[b, 4 * r : 4 * r + 4] = total[b, 4 * r : 4 * r + 4] + part
        for b in range(blocks):
            span = slice(b * 128, (b + 1) * 128)
            shifted = jnp.where(row_ids == 0, halo[b : b + 1], pltpu.roll(depth[b], 1, 0))
            update = total[b] + (shifted - depth[b])
            old = image_ref[:, span]
            image = jnp.maximum(old - primal_step * update, 0.0)
            xbar[b] = 2.0 * image - old
            image_ref[:, span] = image
        return carry

    lax.fori_loop(0, ITERS - 1, iteration, 0)

    spread_bands(lambda g: wave[g], sectors)
    for b in range(blocks):
        for r, part in enumerate(joined_bands(lambda j: j, b)):
            wave_ref[4 * r : 4 * r + 4, b * 128 : (b + 1) * 128] = part

    def drain(i, carry):
        j = far_first(i)
        for it in range(ITERS):
            part_copy(it, j).wait_send()
        for it in range(ITERS - 1):
            share_copy(it, j).wait_send()
        return carry

    lax.fori_loop(0, STOPS - 1, drain, 0)
    for it in range(ITERS - 1):
        edge_copy(it, 0).wait_send()
        edge_copy(it, 1).wait_send()
        for way, source, dest in ((0, bands, tiles), (1, back_bands, wave_back)):
            for offset in range(1, ZS):
                zed_copy(it, way, source, offset).wait_send()
            for offset in range(1, groups):
                group_copy(it, way, dest, offset).wait_send()


def body(measured, tof, tof_rows, tile_owner):
    stops, blocks, slots, width, _ = tof.shape
    depth_rows = measured.shape[0]
    time_blocks = measured.shape[1] // width
    pixels = blocks * width
    sectors = lax.axis_size("sector")
    slabs = lax.axis_size("slab")
    groups = sectors // ZS
    terms = stops * blocks * slots
    met = [HALF] + [far_first(i) for i in range(STOPS - 2, -1, -1)]
    rows = jnp.concatenate([tof_rows[j].reshape(-1) for j in met])
    order = jnp.arange(terms, dtype=jnp.int32)
    wanted = jnp.concatenate([rows, jnp.arange(time_blocks, dtype=jnp.int32)])
    limit = jnp.concatenate([order, jnp.full((time_blocks,), terms, jnp.int32)])
    match = jnp.logical_and(rows[None] == wanted[:, None], order[None] < limit[:, None])
    prev = jnp.max(jnp.where(match, order[None], -1), 1)
    prev = jnp.where(prev < 0, terms, prev)
    bands = jnp.arange(sectors, dtype=jnp.int32)
    inverse = jnp.sum(jnp.where(tile_owner[None] == bands[:, None], bands[None], 0), 1)

    vmem = pl.BlockSpec(memory_space=pltpu.VMEM)
    smem = pl.BlockSpec(memory_space=pltpu.SMEM)
    f32, half = jnp.float32, jnp.bfloat16
    field = (blocks, depth_rows, width)
    again = ITERS - 1
    ring = (groups, ZS, depth_rows // 4, width)
    return pl.pallas_call(
        functools.partial(kernel, sectors, groups, slabs, blocks, time_blocks),
        out_shape=(
            jax.ShapeDtypeStruct((depth_rows, pixels), f32),
            jax.ShapeDtypeStruct(measured.shape, f32),
            jax.ShapeDtypeStruct((depth_rows, pixels), f32),
        ),
        in_specs=[smem] * 4 + [vmem, pl.BlockSpec(memory_space=pl.ANY)],
        out_specs=(vmem, vmem, vmem),
        scratch_shapes=[
            pltpu.VMEM((stops, blocks, slots * width, width), half),
            pltpu.VMEM((terms + 1, depth_rows, width), f32),
            pltpu.VMEM((time_blocks, depth_rows, width), half),
            pltpu.VMEM(field, f32),
            pltpu.VMEM(field, f32),
            pltpu.VMEM((blocks, width), f32),
            pltpu.VMEM(field, f32),
            pltpu.VMEM((again, stops) + field, half),
            pltpu.VMEM((ITERS, stops) + field, half),
            pltpu.VMEM((ITERS, stops) + field, half),
            pltpu.VMEM((again, 2, blocks, width), f32),
            pltpu.VMEM((again, 2, blocks, width), f32),
            pltpu.VMEM((4 * blocks, depth_rows, width), f32),
            pltpu.VMEM((again,) + ring, f32),
            pltpu.VMEM((again, 2) + ring, f32),
            pltpu.VMEM((again,) + ring, f32),
            pltpu.VMEM(ring, f32),
            pltpu.VMEM((4, sectors, depth_rows // 4, width), f32),
            pltpu.VMEM((again,) + ring, f32),
            pltpu.VMEM((again,) + ring, f32),
            pltpu.SemaphoreType.DMA((stops,)),
            pltpu.SemaphoreType.DMA((again, stops)),
            pltpu.SemaphoreType.DMA((again, stops)),
            pltpu.SemaphoreType.DMA((ITERS, stops)),
            pltpu.SemaphoreType.DMA((ITERS, stops)),
            pltpu.SemaphoreType.DMA((again, 2)),
            pltpu.SemaphoreType.DMA((again, 2)),
            pltpu.SemaphoreType.DMA((again, 2, 2, ZS)),
            pltpu.SemaphoreType.DMA((again, 2, 2, ZS)),
        ],
        compiler_params=pltpu.CompilerParams(
            collective_id=0, has_side_effects=True, vmem_limit_bytes=48 * 1024 * 1024
        ),
    )(tof_rows.reshape(-1), prev, tile_owner, inverse, measured, tof.reshape(stops, blocks, slots * width, width))


def solution(mesh):
    return jax.shard_map(
        body,
        mesh=mesh,
        in_specs=(
            P("slab", "sector"),
            P("sector", None, None, None, None),
            P("sector", None, None),
            P(),
        ),
        out_specs=(P("slab", "sector"), P("slab", "sector"), P("slab", "sector")),
        check_vma=False,
    )
```

```python
import functools

import jax
import jax.numpy as jnp
import numpy as np
from jax import lax
from jax.experimental import pallas as pl
from jax.experimental.pallas import tpu as pltpu
from jax.sharding import PartitionSpec as P

ITERS = 3
STOPS = 8
HALF = STOPS // 2
ZS = 8

dual_step = 0.5
primal_step = 0.15
wave_limit = 0.5
depth_limit = 0.5


CHUNKS = 4


def term_place(stop, block, slot, blocks):
    size = blocks // CHUNKS
    chunk, inside = block // size, 2 * (block % size) + slot
    step = abs(stop - HALF)
    if step == 0:
        return 2 * block + slot
    both = step < HALF
    base = 2 * blocks * (2 * step - 1) + chunk * 2 * size * (2 if both else 1)
    return base + (2 * size if stop > HALF else 0) + inside


def kernel(
    sectors, groups, slabs, blocks, time_blocks,
    rows_ref, prev_ref, owner_ref, inverse_ref, measured_ref, tof_hbm,
    image_ref, data_ref, wave_ref,
    tof, sums, dual_half, xbar, depth, halo, total,
    shares, part_out, part_in, last_out, last_in, edge_out, edge_in,
    rolled, bands, mid, tiles, wave, rolled_back, back_bands, wave_back,
    load_sem, share_send, share_recv, part_send, part_recv, last_send, last_recv, edge_send, edge_recv,
    band_send, band_recv,
):
    me = lax.axis_index("sector")
    slab = lax.axis_index("slab")
    group, zed = me // ZS, lax.rem(me, ZS)
    terms = STOPS * blocks * 2
    size = blocks // CHUNKS

    loads = [
        pltpu.make_async_copy(tof_hbm.at[j], tof.at[j], load_sem.at[j]) for j in range(STOPS)
    ]
    for i in (0, 7, 1, 6, 2, 5, 3, 4):
        loads[i].start()

    def sector_at(offset):
        return lax.rem(me + offset + sectors, sectors)

    def group_at(offset):
        return lax.rem(group + offset, groups)

    def zed_at(offset):
        return lax.rem(zed + offset, ZS)

    def slab_at(offset):
        return lax.rem(slab + offset + slabs, slabs)

    barrier = pltpu.get_barrier_semaphore()
    greeted = 0
    for sign in (1, -1):
        pl.semaphore_signal(barrier, inc=1, device_id={"sector": sector_at(sign)})
        greeted += 1
    for offset in range(1, ZS):
        pl.semaphore_signal(barrier, inc=1, device_id={"sector": group * ZS + zed_at(offset)})
        greeted += 1
    for offset in range(1, groups):
        pl.semaphore_signal(barrier, inc=1, device_id={"sector": group_at(offset) * ZS + zed})
        greeted += 1
    for sign in (1, -1):
        pl.semaphore_signal(barrier, inc=1, device_id={"slab": slab_at(sign)})
        greeted += 1

    lanes = lax.broadcasted_iota(jnp.int32, (4, 128), 1)
    quarter = lanes // 32
    odd_lane = lax.rem(lax.broadcasted_iota(jnp.int32, (ZS, 4, 128), 2), 2) == 1
    row_ids = lax.broadcasted_iota(jnp.int32, (16, 128), 0)
    last_slab = slab == slabs - 1
    first_slab = slab == 0

    def share_copy(it, j, c):
        way = 1 if j < HALF else -1
        part = pl.ds(c * size, size)
        return pltpu.make_async_remote_copy(
            src_ref=shares.at[it, j + way, part], dst_ref=shares.at[it, j, part],
            send_sem=share_send.at[it, j, c], recv_sem=share_recv.at[it, j, c],
            device_id={"sector": sector_at(way)},
        )

    def part_copy(it, j, c):
        way = 1 if j > HALF else -1
        part = pl.ds(c * size, size)
        return pltpu.make_async_remote_copy(
            src_ref=part_out.at[it, j, part], dst_ref=part_in.at[it, j, part],
            send_sem=part_send.at[it, j, c], recv_sem=part_recv.at[it, j, c],
            device_id={"sector": sector_at(way)},
        )

    def last_copy(it, side, c):
        part = pl.ds(c * size, size)
        return pltpu.make_async_remote_copy(
            src_ref=last_out.at[it, side, part], dst_ref=last_in.at[it, side, part],
            send_sem=last_send.at[it, side, c], recv_sem=last_recv.at[it, side, c],
            device_id={"sector": sector_at(1 if side else -1)},
        )

    def edge_copy(it, way):
        return pltpu.make_async_remote_copy(
            src_ref=edge_out.at[it, way], dst_ref=edge_in.at[it, way],
            send_sem=edge_send.at[it, way], recv_sem=edge_recv.at[it, way],
            device_id={"slab": slab_at(1 if way else -1)},
        )

    def zed_copy(it, way, source, offset):
        return pltpu.make_async_remote_copy(
            src_ref=source.at[it, :, zed_at(offset)], dst_ref=mid.at[it, way, :, zed],
            send_sem=band_send.at[it, way, 0, offset], recv_sem=band_recv.at[it, way, 0, offset],
            device_id={"sector": group * ZS + zed_at(offset)},
        )

    def zed_wait(it, way, source, offset):
        pltpu.make_async_remote_copy(
            src_ref=source.at[it, :, zed_at(offset)], dst_ref=mid.at[it, way, :, zed_at(ZS - offset)],
            send_sem=band_send.at[it, way, 0, offset], recv_sem=band_recv.at[it, way, 0, offset],
            device_id={"sector": group * ZS + zed_at(offset)},
        ).wait_recv()

    def group_copy(it, way, dest, offset):
        return pltpu.make_async_remote_copy(
            src_ref=mid.at[it, way, group_at(offset)], dst_ref=dest.at[it, group],
            send_sem=band_send.at[it, way, 1, offset], recv_sem=band_recv.at[it, way, 1, offset],
            device_id={"sector": group_at(offset) * ZS + zed},
        )

    def group_wait(it, way, dest, offset):
        pltpu.make_async_remote_copy(
            src_ref=mid.at[it, way, group_at(offset)], dst_ref=dest.at[it, group_at(groups - offset)],
            send_sem=band_send.at[it, way, 1, offset], recv_sem=band_recv.at[it, way, 1, offset],
            device_id={"sector": group_at(offset) * ZS + zed},
        ).wait_recv()

    def first_hop(it, way, source):
        for offset in range(1, ZS):
            zed_copy(it, way, source, offset).start()
        mid[it, way, :, pl.ds(zed, 1)] = source[it, :, pl.ds(zed, 1)]

    def second_hop(it, way, source, dest):
        for offset in range(1, ZS):
            zed_wait(it, way, source, offset)
        for offset in range(1, groups):
            group_copy(it, way, dest, offset).start()
        dest[it, pl.ds(group, 1)] = mid[it, way, pl.ds(group, 1)]

    def finish_hops(it, way, dest):
        for offset in range(1, groups):
            group_wait(it, way, dest, offset)

    def forward_block(it, j, b, place):
        out = lax.dot_general(
            shares[it, j, b], tof[j, b], (((1,), (1,)), ((), ())),
            preferred_element_type=jnp.float32,
        )
        n = j * (2 * blocks) + 2 * b
        sums[place] = out[:, :128] + sums[prev_ref[n]]
        sums[place + 1] = out[:, 128:] + sums[prev_ref[n + 1]]

    def adjoint_block(j, b):
        n = j * (2 * blocks) + 2 * b
        picked = jnp.concatenate([dual_half[rows_ref[n]], dual_half[rows_ref[n + 1]]], 1)
        return jnp.dot(picked, tof[j, b], preferred_element_type=jnp.float32)

    sums[terms] = jnp.zeros((16, 128), jnp.float32)

    for t in range(time_blocks):
        span = slice(t * 128, (t + 1) * 128)
        dual = (dual_step * (0.0 - measured_ref[:, span])) / (1.0 + dual_step)
        data_ref[:, span] = dual
        dual_half[t] = dual.astype(jnp.bfloat16)

    pl.semaphore_wait(barrier, greeted)

    def adjoint_step(it, step, first):
        down, up = step, STOPS - 1 - step
        if first:
            loads[down].wait()
            loads[up].wait()

        def chunk(c, carry):
            lower = [adjoint_block(down, c * size + i) for i in range(size)]
            upper = [adjoint_block(up, c * size + i) for i in range(size)]
            if step > 0:
                part_copy(it, down - 1, c).wait_recv()
                for i in range(size):
                    lower[i] = lower[i] + part_in[it, down - 1, c * size + i].astype(jnp.float32)
            if step < HALF - 1:
                for i in range(size):
                    part_out[it, down, c * size + i] = lower[i].astype(jnp.bfloat16)
                part_copy(it, down, c).start()
            else:
                for i in range(size):
                    last_out[it, 0, c * size + i] = lower[i]
                last_copy(it, 0, c).start()
            if step == HALF - 1:
                for i in range(size):
                    total[c * size + i] = upper[i]
                return carry
            if step > 0:
                part_copy(it, up + 1, c).wait_recv()
                for i in range(size):
                    upper[i] = upper[i] + part_in[it, up + 1, c * size + i].astype(jnp.float32)
            if step < HALF - 2:
                for i in range(size):
                    part_out[it, up, c * size + i] = upper[i].astype(jnp.bfloat16)
                part_copy(it, up, c).start()
            else:
                for i in range(size):
                    last_out[it, 1, c * size + i] = upper[i]
                last_copy(it, 1, c).start()
            return carry

        lax.fori_loop(0, CHUNKS, chunk, 0)

    def back_block(it, b):
        return total[b] + last_in[it, 1, b] + last_in[it, 0, b]

    def arrived(it, c):
        last_copy(it, 1, c).wait_recv()
        last_copy(it, 0, c).wait_recv()

    def forward_own(it):
        def chunk(c, carry):
            for i in range(size):
                b = c * size + i
                forward_block(it, HALF, b, 2 * b)
            return carry

        lax.fori_loop(0, CHUNKS, chunk, 0)

    def forward_step(it, step):
        down, up = HALF + step, HALF - step
        sides = (up, down) if step < HALF else (up,)

        def chunk(c, carry):
            for j in sides:
                share_copy(it, j, c).wait_recv()
                if 0 < j < STOPS - 1:
                    share_copy(it, j + (1 if j > HALF else -1), c).start()
                place = term_place(j, 0, 0, blocks) + c * (2 * size * len(sides))
                for i in range(size):
                    forward_block(it, j, c * size + i, place + 2 * i)
            return carry

        lax.fori_loop(0, CHUNKS, chunk, 0)

    def publish(it):
        for c in range(CHUNKS):
            for b in range(c * size, (c + 1) * size):
                shares[it, HALF, b] = xbar[b].astype(jnp.bfloat16)
            share_copy(it, HALF - 1, c).start()
            share_copy(it, HALF + 1, c).start()
        for b in range(blocks):
            edge_out[it, 0, pl.ds(b, 1)] = xbar[b, 0:1]
            edge_out[it, 1, pl.ds(b, 1)] = xbar[b, 15:16]
        edge_copy(it, 0).start()
        edge_copy(it, 1).start()
        for b in range(blocks):
            value = xbar[b]
            rolled[b] = value
            for a in range(1, 4):
                rolled[a * blocks + b] = pltpu.roll(value, 32 * a, 1)

        def gather_band(k, carry):
            j = inverse_ref[k]
            block, lane = j // 4, lax.rem(j, 4)
            parts = [
                rolled[lax.rem(r - lane + 4, 4) * blocks + block, 4 * r : 4 * r + 4]
                for r in range(4)
            ]
            low = jnp.where(quarter == 0, parts[0], parts[1])
            high = jnp.where(quarter == 2, parts[2], parts[3])
            bands[it, k // ZS, lax.rem(k, ZS)] = jnp.where(quarter < 2, low, high)
            return carry

        lax.fori_loop(0, sectors, gather_band, 0, unroll=8)
        first_hop(it, 0, bands)

    def haar(upper, lower):
        def pairs(value):
            right = pltpu.roll(value, 127, 2)
            left = pltpu.roll(value, 1, 2)
            return jnp.where(odd_lane, left - value, value + right)

        top, low = pairs(upper), pairs(lower)
        return (top + low) * 0.5, (top - low) * 0.5

    def update_wave(it):
        for g in range(groups):
            full = tiles[it, g]
            upper = jnp.concatenate([full[2 * (i // 2)][None] for i in range(ZS)], 0)
            lower = jnp.concatenate([full[2 * (i // 2) + 1][None] for i in range(ZS)], 0)
            odd = lax.rem(lax.broadcasted_iota(jnp.int32, (ZS, 4, 128), 0), 2) == 1
            top, low = haar(upper, lower)
            coeffs = jnp.where(odd, low, top)
            kept = wave[g] + dual_step * coeffs
            dual = jnp.clip(kept, -wave_limit, wave_limit)
            wave[g] = dual
            upper = jnp.concatenate([dual[2 * (i // 2)][None] for i in range(ZS)], 0)
            lower = jnp.concatenate([dual[2 * (i // 2) + 1][None] for i in range(ZS)], 0)
            top, low = haar(upper, lower)
            back_bands[it, g] = jnp.where(odd, low, top)

    def update_depth(it):
        edge_copy(it, 0).wait_recv()
        edge_copy(it, 1).wait_recv()
        following = edge_in[it, 0]
        previous = edge_in[it, 1]
        for b in range(blocks):
            value = xbar[b]
            up = jnp.where(row_ids == 15, following[b : b + 1], pltpu.roll(value, 15, 0))
            diff = up - value
            diff = jnp.where(jnp.logical_and(last_slab, row_ids == 15), 0.0, diff)
            depth[b] = jnp.clip(depth[b] + dual_step * diff, -depth_limit, depth_limit)
        edge = halo[...] + dual_step * (edge_out[it, 0] - previous)
        edge = jnp.clip(edge, -depth_limit, depth_limit)
        halo[...] = jnp.where(first_slab, 0.0, edge)

    def spread_bands(source, count):
        for g in range(count // ZS):
            value = source(g)
            rolled_back[0, pl.ds(g * ZS, ZS)] = value
            for a in range(1, 4):
                rolled_back[a, pl.ds(g * ZS, ZS)] = pltpu.roll(value, 32 * a, 2)

    def joined_bands(index, b):
        places = [index(4 * b + q) for q in range(4)]
        out = []
        for r in range(4):
            parts = [rolled_back[(q - r) % 4, places[q]] for q in range(4)]
            low = jnp.where(quarter == 0, parts[0], parts[1])
            high = jnp.where(quarter == 2, parts[2], parts[3])
            out.append(jnp.where(quarter < 2, low, high))
        return out

    for step in range(HALF):
        adjoint_step(0, step, True)
    for c in range(CHUNKS):
        arrived(0, c)
    for b in range(blocks):
        image = jnp.maximum(0.0 - primal_step * back_block(0, b), 0.0)
        image_ref[:, b * 128 : (b + 1) * 128] = image
        xbar[b] = 2.0 * image
        depth[b] = jnp.zeros((16, 128), jnp.float32)
    halo[...] = jnp.zeros_like(halo)
    wave[...] = jnp.zeros_like(wave)

    def iteration(it, carry):
        publish(it)
        forward_own(it)
        forward_step(it, 1)
        forward_step(it, 2)
        second_hop(it, 0, bands, tiles)
        forward_step(it, 3)
        forward_step(it, 4)
        for t in range(time_blocks):
            span = slice(t * 128, (t + 1) * 128)
            moved = sums[prev_ref[terms + t]] - measured_ref[:, span]
            dual = (data_ref[:, span] + dual_step * moved) / (1.0 + dual_step)
            data_ref[:, span] = dual
            dual_half[t] = dual.astype(jnp.bfloat16)
        adjoint_step(it + 1, 0, False)
        finish_hops(it, 0, tiles)
        update_wave(it)
        first_hop(it, 1, back_bands)
        adjoint_step(it + 1, 1, False)
        update_depth(it)
        adjoint_step(it + 1, 2, False)
        second_hop(it, 1, back_bands, wave_back)
        adjoint_step(it + 1, 3, False)
        finish_hops(it, 1, wave_back)
        spread_bands(lambda g: wave_back[it, g], sectors)
        for b in range(blocks):
            for r, part in enumerate(joined_bands(lambda j: owner_ref[j], b)):
                total[b, 4 * r : 4 * r + 4] = total[b, 4 * r : 4 * r + 4] + part
        for c in range(CHUNKS):
            arrived(it + 1, c)
        for b in range(blocks):
            span = slice(b * 128, (b + 1) * 128)
            shifted = jnp.where(row_ids == 0, halo[b : b + 1], pltpu.roll(depth[b], 1, 0))
            update = back_block(it + 1, b) + (shifted - depth[b])
            old = image_ref[:, span]
            image = jnp.maximum(old - primal_step * update, 0.0)
            xbar[b] = 2.0 * image - old
            image_ref[:, span] = image
        return carry

    lax.fori_loop(0, ITERS - 1, iteration, 0)

    spread_bands(lambda g: wave[g], sectors)
    for b in range(blocks):
        for r, part in enumerate(joined_bands(lambda j: j, b)):
            wave_ref[4 * r : 4 * r + 4, b * 128 : (b + 1) * 128] = part

    def drain(c, carry):
        for j in range(STOPS):
            if j == HALF:
                continue
            for it in range(ITERS - 1):
                share_copy(it, j, c).wait_send()
            if j not in (HALF - 1, HALF + 1):
                for it in range(ITERS):
                    part_copy(it, j, c).wait_send()
        for it in range(ITERS):
            last_copy(it, 0, c).wait_send()
            last_copy(it, 1, c).wait_send()
        return carry

    lax.fori_loop(0, CHUNKS, drain, 0)
    for it in range(ITERS - 1):
        edge_copy(it, 0).wait_send()
        edge_copy(it, 1).wait_send()
        for way, source, dest in ((0, bands, tiles), (1, back_bands, wave_back)):
            for offset in range(1, ZS):
                zed_copy(it, way, source, offset).wait_send()
            for offset in range(1, groups):
                group_copy(it, way, dest, offset).wait_send()


def body(measured, tof, tof_rows, tile_owner):
    stops, blocks, slots, width, _ = tof.shape
    depth_rows = measured.shape[0]
    time_blocks = measured.shape[1] // width
    pixels = blocks * width
    sectors = lax.axis_size("sector")
    slabs = lax.axis_size("slab")
    groups = sectors // ZS
    terms = stops * blocks * slots
    rows = tof_rows.reshape(-1)
    place = np.array(
        [
            term_place(j, b, k, blocks)
            for j in range(stops)
            for b in range(blocks)
            for k in range(slots)
        ],
        np.int32,
    )
    wanted = jnp.concatenate([rows, jnp.arange(time_blocks, dtype=jnp.int32)])
    limit = jnp.asarray(np.concatenate([place, np.full((time_blocks,), terms, np.int32)]))
    place = jnp.asarray(place)
    match = jnp.logical_and(rows[None] == wanted[:, None], place[None] < limit[:, None])
    prev = jnp.max(jnp.where(match, place[None], -1), 1)
    prev = jnp.where(prev < 0, terms, prev)
    bands = jnp.arange(sectors, dtype=jnp.int32)
    inverse = jnp.sum(jnp.where(tile_owner[None] == bands[:, None], bands[None], 0), 1)

    vmem = pl.BlockSpec(memory_space=pltpu.VMEM)
    smem = pl.BlockSpec(memory_space=pltpu.SMEM)
    f32, half = jnp.float32, jnp.bfloat16
    field = (blocks, depth_rows, width)
    again = ITERS - 1
    ring = (groups, ZS, depth_rows // 4, width)
    return pl.pallas_call(
        functools.partial(kernel, sectors, groups, slabs, blocks, time_blocks),
        out_shape=(
            jax.ShapeDtypeStruct((depth_rows, pixels), f32),
            jax.ShapeDtypeStruct(measured.shape, f32),
            jax.ShapeDtypeStruct((depth_rows, pixels), f32),
        ),
        in_specs=[smem] * 4 + [vmem, pl.BlockSpec(memory_space=pl.ANY)],
        out_specs=(vmem, vmem, vmem),
        scratch_shapes=[
            pltpu.VMEM((stops, blocks, slots * width, width), half),
            pltpu.VMEM((terms + 1, depth_rows, width), f32),
            pltpu.VMEM((time_blocks, depth_rows, width), half),
            pltpu.VMEM(field, f32),
            pltpu.VMEM(field, f32),
            pltpu.VMEM((blocks, width), f32),
            pltpu.VMEM(field, f32),
            pltpu.VMEM((again, stops) + field, half),
            pltpu.VMEM((ITERS, stops) + field, half),
            pltpu.VMEM((ITERS, stops) + field, half),
            pltpu.VMEM((ITERS, 2) + field, f32),
            pltpu.VMEM((ITERS, 2) + field, f32),
            pltpu.VMEM((again, 2, blocks, width), f32),
            pltpu.VMEM((again, 2, blocks, width), f32),
            pltpu.VMEM((4 * blocks, depth_rows, width), f32),
            pltpu.VMEM((again,) + ring, f32),
            pltpu.VMEM((again, 2) + ring, f32),
            pltpu.VMEM((again,) + ring, f32),
            pltpu.VMEM(ring, f32),
            pltpu.VMEM((4, sectors, depth_rows // 4, width), f32),
            pltpu.VMEM((again,) + ring, f32),
            pltpu.VMEM((again,) + ring, f32),
            pltpu.SemaphoreType.DMA((stops,)),
            pltpu.SemaphoreType.DMA((again, stops, CHUNKS)),
            pltpu.SemaphoreType.DMA((again, stops, CHUNKS)),
            pltpu.SemaphoreType.DMA((ITERS, stops, CHUNKS)),
            pltpu.SemaphoreType.DMA((ITERS, stops, CHUNKS)),
            pltpu.SemaphoreType.DMA((ITERS, 2, CHUNKS)),
            pltpu.SemaphoreType.DMA((ITERS, 2, CHUNKS)),
            pltpu.SemaphoreType.DMA((again, 2)),
            pltpu.SemaphoreType.DMA((again, 2)),
            pltpu.SemaphoreType.DMA((again, 2, 2, ZS)),
            pltpu.SemaphoreType.DMA((again, 2, 2, ZS)),
        ],
        compiler_params=pltpu.CompilerParams(
            collective_id=0, has_side_effects=True, vmem_limit_bytes=48 * 1024 * 1024
        ),
    )(rows, prev, tile_owner, inverse, measured, tof.reshape(stops, blocks, slots * width, width))


def solution(mesh):
    return jax.shard_map(
        body,
        mesh=mesh,
        in_specs=(
            P("slab", "sector"),
            P("sector", None, None, None, None),
            P("sector", None, None),
            P(),
        ),
        out_specs=(P("slab", "sector"), P("slab", "sector"), P("slab", "sector")),
        check_vma=False,
    )
```

```python
import functools

import jax
import jax.numpy as jnp
from jax import lax
from jax.experimental import pallas as pl
from jax.experimental.pallas import tpu as pltpu
from jax.sharding import PartitionSpec as P

ITERS = 3
STOPS = 8
HALF = STOPS // 2
ZS = 8

dual_step = 0.5
primal_step = 0.15
wave_limit = 0.5
depth_limit = 0.5


MET = (4, 2, 6, 3, 5, 1, 7, 0)
SENT = (0, 1, 7, 3, 5, 2, 6, 4)
HOPS = {0: -2, 1: -1, 7: 1, 3: -1, 5: 1, 2: -2, 6: 2}
UNROLL = 8


def kernel(
    sectors, groups, slabs, blocks, time_blocks,
    rows_ref, owner_ref, rows_block, owner_block, measured_hbm, tof_hbm,
    image_ref, data_ref, wave_ref,
    tof, measured_ref, prev_block, last_block, inverse_block, prev_ref, last_ref, inverse_ref, sums, dual_half, xbar, depth, halo, total,
    shares, part_out, part_in, relay, edge_out, edge_in,
    rolled, bands, mid, tiles, wave, rolled_back, back_bands, wave_back,
    load_sem, index_sem, share_send, share_recv, part_send, part_recv, edge_send, edge_recv,
    band_send, band_recv,
):
    me = lax.axis_index("sector")
    slab = lax.axis_index("slab")
    group, zed = me // ZS, lax.rem(me, ZS)
    terms = STOPS * blocks * 2

    loads = [
        pltpu.make_async_copy(tof_hbm.at[j], tof.at[j], load_sem.at[j]) for j in range(STOPS)
    ]
    measured_load = pltpu.make_async_copy(measured_hbm, measured_ref, load_sem.at[STOPS])
    measured_load.start()
    for j in SENT:
        loads[j].start()

    def sector_at(offset):
        return lax.rem(me + offset + sectors, sectors)

    def group_at(offset):
        return lax.rem(group + offset, groups)

    def zed_at(offset):
        return lax.rem(zed + offset, ZS)

    def slab_at(offset):
        return lax.rem(slab + offset + slabs, slabs)

    barrier = pltpu.get_barrier_semaphore()
    greeted = 0
    for hop in (1, -1, 2, -2):
        pl.semaphore_signal(barrier, inc=1, device_id={"sector": sector_at(hop)})
        greeted += 1
    for offset in range(1, ZS):
        pl.semaphore_signal(barrier, inc=1, device_id={"sector": group * ZS + zed_at(offset)})
        greeted += 1
    for offset in range(1, groups):
        pl.semaphore_signal(barrier, inc=1, device_id={"sector": group_at(offset) * ZS + zed})
        greeted += 1
    for sign in (1, -1):
        pl.semaphore_signal(barrier, inc=1, device_id={"slab": slab_at(sign)})
        greeted += 1

    lanes = lax.broadcasted_iota(jnp.int32, (4, 128), 1)
    quarter = lanes // 32
    odd_lane = lax.rem(lax.broadcasted_iota(jnp.int32, (ZS, 4, 128), 2), 2) == 1
    row_ids = lax.broadcasted_iota(jnp.int32, (16, 128), 0)
    last_slab = slab == slabs - 1
    first_slab = slab == 0

    def share_copy(it, j):
        source = {3: HALF, 5: HALF, 2: HALF, 6: HALF, 1: 2, 0: 2, 7: 6}[j]
        return pltpu.make_async_remote_copy(
            src_ref=shares.at[it, source], dst_ref=shares.at[it, j],
            send_sem=share_send.at[it, j], recv_sem=share_recv.at[it, j],
            device_id={"sector": sector_at(source - j)},
        )

    def part_copy(it, j):
        return pltpu.make_async_remote_copy(
            src_ref=part_out.at[it, j], dst_ref=part_in.at[it, j],
            send_sem=part_send.at[it, j], recv_sem=part_recv.at[it, j],
            device_id={"sector": sector_at(HOPS[j])},
        )

    def edge_copy(it, way):
        return pltpu.make_async_remote_copy(
            src_ref=edge_out.at[it, way], dst_ref=edge_in.at[it, way],
            send_sem=edge_send.at[it, way], recv_sem=edge_recv.at[it, way],
            device_id={"slab": slab_at(1 if way else -1)},
        )

    def zed_copy(it, way, source, offset):
        return pltpu.make_async_remote_copy(
            src_ref=source.at[it, :, zed_at(offset)], dst_ref=mid.at[it, way, :, zed],
            send_sem=band_send.at[it, way, 0, offset], recv_sem=band_recv.at[it, way, 0, offset],
            device_id={"sector": group * ZS + zed_at(offset)},
        )

    def zed_wait(it, way, source, offset):
        pltpu.make_async_remote_copy(
            src_ref=source.at[it, :, zed_at(offset)], dst_ref=mid.at[it, way, :, zed_at(ZS - offset)],
            send_sem=band_send.at[it, way, 0, offset], recv_sem=band_recv.at[it, way, 0, offset],
            device_id={"sector": group * ZS + zed_at(offset)},
        ).wait_recv()

    def group_copy(it, way, dest, offset):
        return pltpu.make_async_remote_copy(
            src_ref=mid.at[it, way, group_at(offset)], dst_ref=dest.at[it, group],
            send_sem=band_send.at[it, way, 1, offset], recv_sem=band_recv.at[it, way, 1, offset],
            device_id={"sector": group_at(offset) * ZS + zed},
        )

    def group_wait(it, way, dest, offset):
        pltpu.make_async_remote_copy(
            src_ref=mid.at[it, way, group_at(offset)], dst_ref=dest.at[it, group_at(groups - offset)],
            send_sem=band_send.at[it, way, 1, offset], recv_sem=band_recv.at[it, way, 1, offset],
            device_id={"sector": group_at(offset) * ZS + zed},
        ).wait_recv()

    def first_hop(it, way, source):
        for offset in range(1, ZS):
            zed_copy(it, way, source, offset).start()
        mid[it, way, :, pl.ds(zed, 1)] = source[it, :, pl.ds(zed, 1)]

    def second_hop(it, way, source, dest):
        for offset in range(1, ZS):
            zed_wait(it, way, source, offset)
        for offset in range(1, groups):
            group_copy(it, way, dest, offset).start()
        dest[it, pl.ds(group, 1)] = mid[it, way, pl.ds(group, 1)]

    def finish_hops(it, way, dest):
        for offset in range(1, groups):
            group_wait(it, way, dest, offset)

    def forward_block(it, j, b, place):
        out = lax.dot_general(
            shares[it, j, b], tof[j, b], (((1,), (1,)), ((), ())),
            preferred_element_type=jnp.float32,
        )
        sums[place] = out[:, :128] + sums[prev_ref[0, place]]
        sums[place + blocks] = out[:, 128:]

    def adjoint_block(j, b):
        picked = jnp.concatenate([dual_half[rows_ref[j, 0, b]], dual_half[rows_ref[j, 1, b]]], 1)
        return jnp.dot(picked, tof[j, b], preferred_element_type=jnp.float32)

    sums[terms] = jnp.zeros((16, 128), jnp.float32)
    measured_load.wait()

    for t in range(time_blocks):
        span = slice(t * 128, (t + 1) * 128)
        dual = (dual_step * (0.0 - measured_ref[:, span])) / (1.0 + dual_step)
        data_ref[:, span] = dual
        dual_half[t] = dual.astype(jnp.bfloat16)

    pl.semaphore_wait(barrier, greeted)

    def each_block(work):
        def some(i, carry):
            for k in range(UNROLL):
                work(i * UNROLL + k)
            return carry

        lax.fori_loop(0, blocks // UNROLL, some, 0)

    def adjoint_stop(it, j, first):
        if first:
            loads[j].wait()

        def work(b):
            value = adjoint_block(j, b)
            if j == HALF:
                total[b] = value
            elif j in (2, 6):
                relay[j // 4, b] = value
            else:
                part_out[it, j, b] = value.astype(jnp.bfloat16)

        each_block(work)
        if j not in (HALF, 2, 6):
            part_copy(it, j).start()

    def adjoint_relay(it, j):
        arrivals = (0, 1) if j == 2 else (7,)
        for k in arrivals:
            part_copy(it, k).wait_recv()
        for b in range(blocks):
            value = relay[j // 4, b]
            for k in arrivals:
                value = value + part_in[it, k, b].astype(jnp.float32)
            part_out[it, j, b] = value.astype(jnp.bfloat16)
        part_copy(it, j).start()

    def back_block(it, b):
        value = total[b]
        for j in (3, 5, 6, 2):
            value = value + part_in[it, j, b].astype(jnp.float32)
        return value

    def arrived(it):
        for j in (3, 5, 6, 2):
            part_copy(it, j).wait_recv()

    def forward_stop(it, j):
        start = MET.index(j) * 2 * blocks
        each_block(lambda b: forward_block(it, j, b, start + b))
        for place in range(start + blocks, start + 2 * blocks):
            sums[place] = sums[place] + sums[prev_ref[0, place]]

    index_copies = [
        pltpu.make_async_copy(prev_block, prev_ref, index_sem.at[0]),
        pltpu.make_async_copy(last_block, last_ref, index_sem.at[1]),
        pltpu.make_async_copy(inverse_block, inverse_ref, index_sem.at[2]),
    ]

    def index_terms():
        flat = jnp.concatenate([rows_block[j, k : k + 1, :] for j in MET for k in range(2)], 1)
        shape = (time_blocks, terms)
        same = flat == lax.broadcasted_iota(jnp.int32, shape, 0)
        place = lax.broadcasted_iota(jnp.int32, shape, 1)
        seen = jnp.where(same, place, -1)
        span = 1
        while span < terms:
            moved = jnp.where(place >= span, pltpu.roll(seen, span, 1), -1)
            seen = jnp.maximum(seen, moved)
            span *= 2
        before = jnp.where(place >= 1, pltpu.roll(seen, 1, 1), -1)
        prev = jnp.max(jnp.where(same, before, -1), 0, keepdims=True)
        prev_block[...] = jnp.where(prev < 0, terms, prev)
        last = jnp.max(seen, 1, keepdims=True)
        last_block[...] = jnp.broadcast_to(jnp.where(last < 0, terms, last), last_block.shape)
        shape = (sectors, sectors)
        owned = owner_block[...] == lax.broadcasted_iota(jnp.int32, shape, 0)
        inverse = jnp.max(
            jnp.where(owned, lax.broadcasted_iota(jnp.int32, shape, 1), 0), 1, keepdims=True
        )
        inverse_block[...] = jnp.broadcast_to(inverse, inverse_block.shape)
        for copy in index_copies:
            copy.start()

    def publish(it):
        for b in range(blocks):
            shares[it, HALF, b] = xbar[b].astype(jnp.bfloat16)
        for j in (2, 6, 3, 5):
            share_copy(it, j).start()
        for b in range(blocks):
            edge_out[it, 0, pl.ds(b, 1)] = xbar[b, 0:1]
            edge_out[it, 1, pl.ds(b, 1)] = xbar[b, 15:16]
        edge_copy(it, 0).start()
        edge_copy(it, 1).start()
        for b in range(blocks):
            value = xbar[b]
            rolled[b] = value
            for a in range(1, 4):
                rolled[a * blocks + b] = pltpu.roll(value, 32 * a, 1)

        def gather_band(k, carry):
            j = inverse_ref[k, 0]
            block, lane = j // 4, lax.rem(j, 4)
            parts = [
                rolled[lax.rem(r - lane + 4, 4) * blocks + block, 4 * r : 4 * r + 4]
                for r in range(4)
            ]
            low = jnp.where(quarter == 0, parts[0], parts[1])
            high = jnp.where(quarter == 2, parts[2], parts[3])
            bands[it, k // ZS, lax.rem(k, ZS)] = jnp.where(quarter < 2, low, high)
            return carry

        lax.fori_loop(0, sectors, gather_band, 0, unroll=8)
        first_hop(it, 0, bands)

    def haar(upper, lower):
        def pairs(value):
            right = pltpu.roll(value, 127, 2)
            left = pltpu.roll(value, 1, 2)
            return jnp.where(odd_lane, left - value, value + right)

        top, low = pairs(upper), pairs(lower)
        return (top + low) * 0.5, (top - low) * 0.5

    def update_wave(it):
        for g in range(groups):
            full = tiles[it, g]
            upper = jnp.concatenate([full[2 * (i // 2)][None] for i in range(ZS)], 0)
            lower = jnp.concatenate([full[2 * (i // 2) + 1][None] for i in range(ZS)], 0)
            odd = lax.rem(lax.broadcasted_iota(jnp.int32, (ZS, 4, 128), 0), 2) == 1
            top, low = haar(upper, lower)
            coeffs = jnp.where(odd, low, top)
            kept = wave[g] + dual_step * coeffs
            dual = jnp.clip(kept, -wave_limit, wave_limit)
            wave[g] = dual
            upper = jnp.concatenate([dual[2 * (i // 2)][None] for i in range(ZS)], 0)
            lower = jnp.concatenate([dual[2 * (i // 2) + 1][None] for i in range(ZS)], 0)
            top, low = haar(upper, lower)
            back_bands[it, g] = jnp.where(odd, low, top)

    def update_depth(it):
        edge_copy(it, 0).wait_recv()
        edge_copy(it, 1).wait_recv()
        following = edge_in[it, 0]
        previous = edge_in[it, 1]
        for b in range(blocks):
            value = xbar[b]
            up = jnp.where(row_ids == 15, following[b : b + 1], pltpu.roll(value, 15, 0))
            diff = up - value
            diff = jnp.where(jnp.logical_and(last_slab, row_ids == 15), 0.0, diff)
            depth[b] = jnp.clip(depth[b] + dual_step * diff, -depth_limit, depth_limit)
        edge = halo[...] + dual_step * (edge_out[it, 0] - previous)
        edge = jnp.clip(edge, -depth_limit, depth_limit)
        halo[...] = jnp.where(first_slab, 0.0, edge)

    def spread_bands(source, count):
        for g in range(count // ZS):
            value = source(g)
            rolled_back[0, pl.ds(g * ZS, ZS)] = value
            for a in range(1, 4):
                rolled_back[a, pl.ds(g * ZS, ZS)] = pltpu.roll(value, 32 * a, 2)

    def joined_bands(index, b):
        places = [index(4 * b + q) for q in range(4)]
        out = []
        for r in range(4):
            parts = [rolled_back[(q - r) % 4, places[q]] for q in range(4)]
            low = jnp.where(quarter == 0, parts[0], parts[1])
            high = jnp.where(quarter == 2, parts[2], parts[3])
            out.append(jnp.where(quarter < 2, low, high))
        return out

    for j in SENT:
        adjoint_stop(0, j, True)
    index_terms()
    adjoint_relay(0, 6)
    adjoint_relay(0, 2)
    for copy in index_copies:
        copy.wait()
    arrived(0)
    for b in range(blocks):
        image = jnp.maximum(0.0 - primal_step * back_block(0, b), 0.0)
        image_ref[:, b * 128 : (b + 1) * 128] = image
        xbar[b] = 2.0 * image
        depth[b] = jnp.zeros((16, 128), jnp.float32)
    halo[...] = jnp.zeros_like(halo)
    wave[...] = jnp.zeros_like(wave)

    def iteration(it, carry):
        publish(it)
        forward_stop(it, HALF)
        share_copy(it, 2).wait_recv()
        share_copy(it, 0).start()
        share_copy(it, 1).start()
        share_copy(it, 6).wait_recv()
        share_copy(it, 7).start()
        second_hop(it, 0, bands, tiles)
        forward_stop(it, 2)
        forward_stop(it, 6)
        for j in (3, 5, 1, 7, 0):
            share_copy(it, j).wait_recv()
            forward_stop(it, j)
        for t in range(time_blocks):
            span = slice(t * 128, (t + 1) * 128)
            moved = sums[last_ref[t, 0]] - measured_ref[:, span]
            dual = (data_ref[:, span] + dual_step * moved) / (1.0 + dual_step)
            data_ref[:, span] = dual
            dual_half[t] = dual.astype(jnp.bfloat16)
        for j in SENT:
            adjoint_stop(it + 1, j, False)
        finish_hops(it, 0, tiles)
        update_wave(it)
        first_hop(it, 1, back_bands)
        update_depth(it)
        adjoint_relay(it + 1, 6)
        adjoint_relay(it + 1, 2)
        second_hop(it, 1, back_bands, wave_back)
        finish_hops(it, 1, wave_back)
        spread_bands(lambda g: wave_back[it, g], sectors)
        for b in range(blocks):
            for r, part in enumerate(joined_bands(lambda j: owner_ref[j], b)):
                total[b, 4 * r : 4 * r + 4] = total[b, 4 * r : 4 * r + 4] + part
        arrived(it + 1)
        for b in range(blocks):
            span = slice(b * 128, (b + 1) * 128)
            shifted = jnp.where(row_ids == 0, halo[b : b + 1], pltpu.roll(depth[b], 1, 0))
            update = back_block(it + 1, b) + (shifted - depth[b])
            old = image_ref[:, span]
            image = jnp.maximum(old - primal_step * update, 0.0)
            xbar[b] = 2.0 * image - old
            image_ref[:, span] = image
        return carry

    lax.fori_loop(0, ITERS - 1, iteration, 0)

    spread_bands(lambda g: wave[g], sectors)
    for b in range(blocks):
        for r, part in enumerate(joined_bands(lambda j: j, b)):
            wave_ref[4 * r : 4 * r + 4, b * 128 : (b + 1) * 128] = part

    for j in range(STOPS):
        if j != HALF:
            for it in range(ITERS - 1):
                share_copy(it, j).wait_send()
            for it in range(ITERS):
                part_copy(it, j).wait_send()
    for it in range(ITERS - 1):
        edge_copy(it, 0).wait_send()
        edge_copy(it, 1).wait_send()
        for way, source, dest in ((0, bands, tiles), (1, back_bands, wave_back)):
            for offset in range(1, ZS):
                zed_copy(it, way, source, offset).wait_send()
            for offset in range(1, groups):
                group_copy(it, way, dest, offset).wait_send()


def body(measured, tof, tof_rows, tile_owner):
    stops, blocks, slots, width, _ = tof.shape
    depth_rows = measured.shape[0]
    time_blocks = measured.shape[1] // width
    pixels = blocks * width
    sectors = lax.axis_size("sector")
    slabs = lax.axis_size("slab")
    groups = sectors // ZS
    terms = stops * blocks * slots
    rows = tof_rows.transpose(0, 2, 1)
    vmem = pl.BlockSpec(memory_space=pltpu.VMEM)
    smem = pl.BlockSpec(memory_space=pltpu.SMEM)
    f32, half, i32 = jnp.float32, jnp.bfloat16, jnp.int32
    field = (blocks, depth_rows, width)
    again = ITERS - 1
    ring = (groups, ZS, depth_rows // 4, width)
    return pl.pallas_call(
        functools.partial(kernel, sectors, groups, slabs, blocks, time_blocks),
        out_shape=(
            jax.ShapeDtypeStruct((depth_rows, pixels), f32),
            jax.ShapeDtypeStruct(measured.shape, f32),
            jax.ShapeDtypeStruct((depth_rows, pixels), f32),
        ),
        in_specs=[smem, smem, vmem, vmem] + [pl.BlockSpec(memory_space=pl.ANY)] * 2,
        out_specs=(vmem, vmem, vmem),
        scratch_shapes=[
            pltpu.VMEM((stops, blocks, slots * width, width), half),
            pltpu.VMEM(measured.shape, f32),
            pltpu.VMEM((1, terms), i32),
            pltpu.VMEM((time_blocks, width), i32),
            pltpu.VMEM((sectors, width), i32),
            pltpu.SMEM((1, terms), i32),
            pltpu.SMEM((time_blocks, width), i32),
            pltpu.SMEM((sectors, width), i32),
            pltpu.VMEM((terms + 1, depth_rows, width), f32),
            pltpu.VMEM((time_blocks, depth_rows, width), half),
            pltpu.VMEM(field, f32),
            pltpu.VMEM(field, f32),
            pltpu.VMEM((blocks, width), f32),
            pltpu.VMEM(field, f32),
            pltpu.VMEM((again, stops) + field, half),
            pltpu.VMEM((ITERS, stops) + field, half),
            pltpu.VMEM((ITERS, stops) + field, half),
            pltpu.VMEM((2,) + field, f32),
            pltpu.VMEM((again, 2, blocks, width), f32),
            pltpu.VMEM((again, 2, blocks, width), f32),
            pltpu.VMEM((4 * blocks, depth_rows, width), f32),
            pltpu.VMEM((again,) + ring, f32),
            pltpu.VMEM((again, 2) + ring, f32),
            pltpu.VMEM((again,) + ring, f32),
            pltpu.VMEM(ring, f32),
            pltpu.VMEM((4, sectors, depth_rows // 4, width), f32),
            pltpu.VMEM((again,) + ring, f32),
            pltpu.VMEM((again,) + ring, f32),
            pltpu.SemaphoreType.DMA((stops + 1,)),
            pltpu.SemaphoreType.DMA((3,)),
            pltpu.SemaphoreType.DMA((again, stops)),
            pltpu.SemaphoreType.DMA((again, stops)),
            pltpu.SemaphoreType.DMA((ITERS, stops)),
            pltpu.SemaphoreType.DMA((ITERS, stops)),
            pltpu.SemaphoreType.DMA((again, 2)),
            pltpu.SemaphoreType.DMA((again, 2)),
            pltpu.SemaphoreType.DMA((again, 2, 2, ZS)),
            pltpu.SemaphoreType.DMA((again, 2, 2, ZS)),
        ],
        compiler_params=pltpu.CompilerParams(
            collective_id=0, has_side_effects=True, vmem_limit_bytes=60 * 1024 * 1024
        ),
    )(rows, tile_owner, rows, tile_owner[None], measured, tof.reshape(stops, blocks, slots * width, width))


def solution(mesh):
    return jax.shard_map(
        body,
        mesh=mesh,
        in_specs=(
            P("slab", "sector"),
            P("sector", None, None, None, None),
            P("sector", None, None),
            P(),
        ),
        out_specs=(P("slab", "sector"), P("slab", "sector"), P("slab", "sector")),
        check_vma=False,
    )
```

```python
import functools

import jax
import jax.numpy as jnp
from jax import lax
from jax.experimental import pallas as pl
from jax.experimental.pallas import tpu as pltpu
from jax.sharding import PartitionSpec as P

ITERS = 3
STOPS = 8
HALF = STOPS // 2
ZS = 8

dual_step = 0.5
primal_step = 0.15
wave_limit = 0.5
depth_limit = 0.5


MET = (4, 2, 6, 3, 5, 1, 7, 0)
SENT = (0, 1, 7, 3, 5, 2, 6, 4)
HOPS = {0: -2, 1: -1, 7: 1, 3: -1, 5: 1, 2: -2, 6: 2}
UNROLL = 16


def kernel(
    sectors, groups, slabs, blocks, time_blocks,
    rows_ref, owner_ref, rows_block, owner_block, measured_hbm, tof_hbm,
    image_ref, data_ref, wave_ref,
    tof, measured_ref, prev_block, last_block, inverse_block, prev_ref, last_ref, inverse_ref, sums, dual_half, xbar, depth, halo, total,
    shares, part_out, part_in, relay, edge_out, edge_in,
    rolled, bands, mid, tiles, wave, rolled_back, back_bands, wave_back,
    load_sem, index_sem, share_send, share_recv, part_send, part_recv, edge_send, edge_recv,
    band_send, band_recv,
):
    me = lax.axis_index("sector")
    slab = lax.axis_index("slab")
    group, zed = me // ZS, lax.rem(me, ZS)
    terms = STOPS * blocks * 2

    loads = [
        pltpu.make_async_copy(tof_hbm.at[j], tof.at[j], load_sem.at[j]) for j in range(STOPS)
    ]
    measured_load = pltpu.make_async_copy(measured_hbm, measured_ref, load_sem.at[STOPS])
    measured_load.start()
    for j in SENT:
        loads[j].start()

    def sector_at(offset):
        return lax.rem(me + offset + sectors, sectors)

    def group_at(offset):
        return lax.rem(group + offset, groups)

    def zed_at(offset):
        return lax.rem(zed + offset, ZS)

    def slab_at(offset):
        return lax.rem(slab + offset + slabs, slabs)

    barrier = pltpu.get_barrier_semaphore()
    greeted = 0
    for hop in (1, -1, 2, -2):
        pl.semaphore_signal(barrier, inc=1, device_id={"sector": sector_at(hop)})
        greeted += 1
    for offset in range(1, ZS):
        pl.semaphore_signal(barrier, inc=1, device_id={"sector": group * ZS + zed_at(offset)})
        greeted += 1
    for offset in range(1, groups):
        pl.semaphore_signal(barrier, inc=1, device_id={"sector": group_at(offset) * ZS + zed})
        greeted += 1
    for sign in (1, -1):
        pl.semaphore_signal(barrier, inc=1, device_id={"slab": slab_at(sign)})
        greeted += 1

    lanes = lax.broadcasted_iota(jnp.int32, (4, 128), 1)
    quarter = lanes // 32
    odd_lane = lax.rem(lax.broadcasted_iota(jnp.int32, (ZS, 4, 128), 2), 2) == 1
    row_ids = lax.broadcasted_iota(jnp.int32, (16, 128), 0)
    last_slab = slab == slabs - 1
    first_slab = slab == 0

    def share_copy(it, j):
        source = {3: HALF, 5: HALF, 2: HALF, 6: HALF, 1: 2, 0: 2, 7: 6}[j]
        return pltpu.make_async_remote_copy(
            src_ref=shares.at[it, source], dst_ref=shares.at[it, j],
            send_sem=share_send.at[it, j], recv_sem=share_recv.at[it, j],
            device_id={"sector": sector_at(source - j)},
        )

    def part_copy(it, j):
        return pltpu.make_async_remote_copy(
            src_ref=part_out.at[it, j], dst_ref=part_in.at[it, j],
            send_sem=part_send.at[it, j], recv_sem=part_recv.at[it, j],
            device_id={"sector": sector_at(HOPS[j])},
        )

    def edge_copy(it, way):
        return pltpu.make_async_remote_copy(
            src_ref=edge_out.at[it, way], dst_ref=edge_in.at[it, way],
            send_sem=edge_send.at[it, way], recv_sem=edge_recv.at[it, way],
            device_id={"slab": slab_at(1 if way else -1)},
        )

    def zed_copy(it, way, source, offset):
        return pltpu.make_async_remote_copy(
            src_ref=source.at[it, :, zed_at(offset)], dst_ref=mid.at[it, way, :, zed],
            send_sem=band_send.at[it, way, 0, offset], recv_sem=band_recv.at[it, way, 0, offset],
            device_id={"sector": group * ZS + zed_at(offset)},
        )

    def zed_wait(it, way, source, offset):
        pltpu.make_async_remote_copy(
            src_ref=source.at[it, :, zed_at(offset)], dst_ref=mid.at[it, way, :, zed_at(ZS - offset)],
            send_sem=band_send.at[it, way, 0, offset], recv_sem=band_recv.at[it, way, 0, offset],
            device_id={"sector": group * ZS + zed_at(offset)},
        ).wait_recv()

    def group_copy(it, way, dest, offset):
        return pltpu.make_async_remote_copy(
            src_ref=mid.at[it, way, group_at(offset)], dst_ref=dest.at[it, group],
            send_sem=band_send.at[it, way, 1, offset], recv_sem=band_recv.at[it, way, 1, offset],
            device_id={"sector": group_at(offset) * ZS + zed},
        )

    def group_wait(it, way, dest, offset):
        pltpu.make_async_remote_copy(
            src_ref=mid.at[it, way, group_at(offset)], dst_ref=dest.at[it, group_at(groups - offset)],
            send_sem=band_send.at[it, way, 1, offset], recv_sem=band_recv.at[it, way, 1, offset],
            device_id={"sector": group_at(offset) * ZS + zed},
        ).wait_recv()

    def first_hop(it, way, source):
        for offset in range(1, ZS):
            zed_copy(it, way, source, offset).start()
        mid[it, way, :, pl.ds(zed, 1)] = source[it, :, pl.ds(zed, 1)]

    def second_hop(it, way, source, dest):
        for offset in range(1, ZS):
            zed_wait(it, way, source, offset)
        for offset in range(1, groups):
            group_copy(it, way, dest, offset).start()
        dest[it, pl.ds(group, 1)] = mid[it, way, pl.ds(group, 1)]

    def finish_hops(it, way, dest):
        for offset in range(1, groups):
            group_wait(it, way, dest, offset)

    def forward_block(it, j, b, place):
        out = lax.dot_general(
            shares[it, j, b], tof[j, b], (((1,), (1,)), ((), ())),
            preferred_element_type=jnp.float32,
        )
        sums[place] = out[:, :128] + sums[prev_ref[0, place]]
        sums[place + blocks] = out[:, 128:]

    def adjoint_block(j, b):
        picked = jnp.concatenate([dual_half[rows_ref[j, 0, b]], dual_half[rows_ref[j, 1, b]]], 1)
        return jnp.dot(picked, tof[j, b], preferred_element_type=jnp.float32)

    sums[terms] = jnp.zeros((16, 128), jnp.float32)
    measured_load.wait()

    for t in range(time_blocks):
        span = slice(t * 128, (t + 1) * 128)
        dual = (dual_step * (0.0 - measured_ref[:, span])) / (1.0 + dual_step)
        data_ref[:, span] = dual
        dual_half[t] = dual.astype(jnp.bfloat16)

    pl.semaphore_wait(barrier, greeted)

    def each_block(work):
        def some(i, carry):
            for k in range(UNROLL):
                work(i * UNROLL + k)
            return carry

        lax.fori_loop(0, blocks // UNROLL, some, 0)

    def adjoint_stop(it, j, first):
        if first:
            loads[j].wait()

        def work(b):
            value = adjoint_block(j, b)
            if j == HALF:
                total[b] = value
            elif j in (2, 6):
                relay[j // 4, b] = value
            else:
                part_out[it, j, b] = value.astype(jnp.bfloat16)

        each_block(work)
        if j not in (HALF, 2, 6):
            part_copy(it, j).start()

    def adjoint_relay(it, j):
        arrivals = (0, 1) if j == 2 else (7,)
        for k in arrivals:
            part_copy(it, k).wait_recv()
        for b in range(blocks):
            value = relay[j // 4, b]
            for k in arrivals:
                value = value + part_in[it, k, b].astype(jnp.float32)
            part_out[it, j, b] = value.astype(jnp.bfloat16)
        part_copy(it, j).start()

    def back_block(it, b):
        value = total[b]
        for j in (3, 5, 6, 2):
            value = value + part_in[it, j, b].astype(jnp.float32)
        return value

    def arrived(it):
        for j in (3, 5, 6, 2):
            part_copy(it, j).wait_recv()

    def forward_stop(it, j):
        start = MET.index(j) * 2 * blocks
        each_block(lambda b: forward_block(it, j, b, start + b))
        for place in range(start + blocks, start + 2 * blocks):
            sums[place] = sums[place] + sums[prev_ref[0, place]]

    index_copies = [
        pltpu.make_async_copy(prev_block, prev_ref, index_sem.at[0]),
        pltpu.make_async_copy(last_block, last_ref, index_sem.at[1]),
        pltpu.make_async_copy(inverse_block, inverse_ref, index_sem.at[2]),
    ]

    def index_terms():
        flat = jnp.concatenate([rows_block[j, k : k + 1, :] for j in MET for k in range(2)], 1)
        shape = (time_blocks, terms)
        same = flat == lax.broadcasted_iota(jnp.int32, shape, 0)
        place = lax.broadcasted_iota(jnp.int32, shape, 1)
        seen = jnp.where(same, place, -1)
        span = 1
        while span < terms:
            moved = jnp.where(place >= span, pltpu.roll(seen, span, 1), -1)
            seen = jnp.maximum(seen, moved)
            span *= 2
        before = jnp.where(place >= 1, pltpu.roll(seen, 1, 1), -1)
        prev = jnp.max(jnp.where(same, before, -1), 0, keepdims=True)
        prev_block[...] = jnp.where(prev < 0, terms, prev)
        last = jnp.max(seen, 1, keepdims=True)
        last_block[...] = jnp.broadcast_to(jnp.where(last < 0, terms, last), last_block.shape)
        shape = (sectors, sectors)
        owned = owner_block[...] == lax.broadcasted_iota(jnp.int32, shape, 0)
        inverse = jnp.max(
            jnp.where(owned, lax.broadcasted_iota(jnp.int32, shape, 1), 0), 1, keepdims=True
        )
        inverse_block[...] = jnp.broadcast_to(inverse, inverse_block.shape)
        for copy in index_copies:
            copy.start()

    def publish(it):
        for b in range(blocks):
            shares[it, HALF, b] = xbar[b].astype(jnp.bfloat16)
        for j in (2, 6, 3, 5):
            share_copy(it, j).start()
        for b in range(blocks):
            edge_out[it, 0, pl.ds(b, 1)] = xbar[b, 0:1]
            edge_out[it, 1, pl.ds(b, 1)] = xbar[b, 15:16]
        edge_copy(it, 0).start()
        edge_copy(it, 1).start()
        for b in range(blocks):
            value = xbar[b]
            rolled[b] = value
            for a in range(1, 4):
                rolled[a * blocks + b] = pltpu.roll(value, 32 * a, 1)

        def gather_band(k, carry):
            j = inverse_ref[k, 0]
            block, lane = j // 4, lax.rem(j, 4)
            parts = [
                rolled[lax.rem(r - lane + 4, 4) * blocks + block, 4 * r : 4 * r + 4]
                for r in range(4)
            ]
            low = jnp.where(quarter == 0, parts[0], parts[1])
            high = jnp.where(quarter == 2, parts[2], parts[3])
            bands[it, k // ZS, lax.rem(k, ZS)] = jnp.where(quarter < 2, low, high)
            return carry

        lax.fori_loop(0, sectors, gather_band, 0, unroll=8)
        first_hop(it, 0, bands)

    def haar(upper, lower):
        def pairs(value):
            right = pltpu.roll(value, 127, 2)
            left = pltpu.roll(value, 1, 2)
            return jnp.where(odd_lane, left - value, value + right)

        top, low = pairs(upper), pairs(lower)
        return (top + low) * 0.5, (top - low) * 0.5

    def update_wave(it):
        for g in range(groups):
            full = tiles[it, g]
            upper = jnp.concatenate([full[2 * (i // 2)][None] for i in range(ZS)], 0)
            lower = jnp.concatenate([full[2 * (i // 2) + 1][None] for i in range(ZS)], 0)
            odd = lax.rem(lax.broadcasted_iota(jnp.int32, (ZS, 4, 128), 0), 2) == 1
            top, low = haar(upper, lower)
            coeffs = jnp.where(odd, low, top)
            kept = wave[g] + dual_step * coeffs
            dual = jnp.clip(kept, -wave_limit, wave_limit)
            wave[g] = dual
            upper = jnp.concatenate([dual[2 * (i // 2)][None] for i in range(ZS)], 0)
            lower = jnp.concatenate([dual[2 * (i // 2) + 1][None] for i in range(ZS)], 0)
            top, low = haar(upper, lower)
            back_bands[it, g] = jnp.where(odd, low, top)

    def update_depth(it):
        edge_copy(it, 0).wait_recv()
        edge_copy(it, 1).wait_recv()
        following = edge_in[it, 0]
        previous = edge_in[it, 1]
        for b in range(blocks):
            value = xbar[b]
            up = jnp.where(row_ids == 15, following[b : b + 1], pltpu.roll(value, 15, 0))
            diff = up - value
            diff = jnp.where(jnp.logical_and(last_slab, row_ids == 15), 0.0, diff)
            depth[b] = jnp.clip(depth[b] + dual_step * diff, -depth_limit, depth_limit)
        edge = halo[...] + dual_step * (edge_out[it, 0] - previous)
        edge = jnp.clip(edge, -depth_limit, depth_limit)
        halo[...] = jnp.where(first_slab, 0.0, edge)

    def spread_bands(source, count):
        for g in range(count // ZS):
            value = source(g)
            rolled_back[0, pl.ds(g * ZS, ZS)] = value
            for a in range(1, 4):
                rolled_back[a, pl.ds(g * ZS, ZS)] = pltpu.roll(value, 32 * a, 2)

    def joined_bands(index, b):
        places = [index(4 * b + q) for q in range(4)]
        out = []
        for r in range(4):
            parts = [rolled_back[(q - r) % 4, places[q]] for q in range(4)]
            low = jnp.where(quarter == 0, parts[0], parts[1])
            high = jnp.where(quarter == 2, parts[2], parts[3])
            out.append(jnp.where(quarter < 2, low, high))
        return out

    for j in SENT:
        adjoint_stop(0, j, True)
    index_terms()
    adjoint_relay(0, 6)
    adjoint_relay(0, 2)
    for copy in index_copies:
        copy.wait()
    arrived(0)
    for b in range(blocks):
        image = jnp.maximum(0.0 - primal_step * back_block(0, b), 0.0)
        image_ref[:, b * 128 : (b + 1) * 128] = image
        xbar[b] = 2.0 * image
        depth[b] = jnp.zeros((16, 128), jnp.float32)
    halo[...] = jnp.zeros_like(halo)
    wave[...] = jnp.zeros_like(wave)

    def iteration(it, carry):
        publish(it)
        forward_stop(it, HALF)
        share_copy(it, 2).wait_recv()
        share_copy(it, 0).start()
        share_copy(it, 1).start()
        share_copy(it, 6).wait_recv()
        share_copy(it, 7).start()
        second_hop(it, 0, bands, tiles)
        forward_stop(it, 2)
        forward_stop(it, 6)
        for j in (3, 5):
            share_copy(it, j).wait_recv()
            forward_stop(it, j)
        finish_hops(it, 0, tiles)
        update_wave(it)
        first_hop(it, 1, back_bands)
        update_depth(it)
        for j in (1, 7, 0):
            share_copy(it, j).wait_recv()
            forward_stop(it, j)
        for t in range(time_blocks):
            span = slice(t * 128, (t + 1) * 128)
            moved = sums[last_ref[t, 0]] - measured_ref[:, span]
            dual = (data_ref[:, span] + dual_step * moved) / (1.0 + dual_step)
            data_ref[:, span] = dual
            dual_half[t] = dual.astype(jnp.bfloat16)
        for j in SENT:
            adjoint_stop(it + 1, j, False)
        second_hop(it, 1, back_bands, wave_back)
        adjoint_relay(it + 1, 6)
        adjoint_relay(it + 1, 2)
        finish_hops(it, 1, wave_back)
        spread_bands(lambda g: wave_back[it, g], sectors)
        for b in range(blocks):
            for r, part in enumerate(joined_bands(lambda j: owner_ref[j], b)):
                total[b, 4 * r : 4 * r + 4] = total[b, 4 * r : 4 * r + 4] + part
        arrived(it + 1)
        for b in range(blocks):
            span = slice(b * 128, (b + 1) * 128)
            shifted = jnp.where(row_ids == 0, halo[b : b + 1], pltpu.roll(depth[b], 1, 0))
            update = back_block(it + 1, b) + (shifted - depth[b])
            old = image_ref[:, span]
            image = jnp.maximum(old - primal_step * update, 0.0)
            xbar[b] = 2.0 * image - old
            image_ref[:, span] = image
        return carry

    lax.fori_loop(0, ITERS - 1, iteration, 0)

    spread_bands(lambda g: wave[g], sectors)
    for b in range(blocks):
        for r, part in enumerate(joined_bands(lambda j: j, b)):
            wave_ref[4 * r : 4 * r + 4, b * 128 : (b + 1) * 128] = part

    for j in range(STOPS):
        if j != HALF:
            for it in range(ITERS - 1):
                share_copy(it, j).wait_send()
            for it in range(ITERS):
                part_copy(it, j).wait_send()
    for it in range(ITERS - 1):
        edge_copy(it, 0).wait_send()
        edge_copy(it, 1).wait_send()
        for way, source, dest in ((0, bands, tiles), (1, back_bands, wave_back)):
            for offset in range(1, ZS):
                zed_copy(it, way, source, offset).wait_send()
            for offset in range(1, groups):
                group_copy(it, way, dest, offset).wait_send()


def deliver(a, b, c, a_out, b_out, c_out, a_held, b_held, c_held, sem):
    ways = ((a, a_held, a_out), (b, b_held, b_out), (c, c_held, c_out))
    loads = [pltpu.make_async_copy(w[0], w[1], sem.at[0, i]) for i, w in enumerate(ways)]
    stores = [pltpu.make_async_copy(w[1], w[2], sem.at[1, i]) for i, w in enumerate(ways)]
    for load in loads:
        load.start()
    for load, store in zip(loads, stores):
        load.wait()
        store.start()
    for store in stores:
        store.wait()


def body(measured, tof, tof_rows, tile_owner):
    stops, blocks, slots, width, _ = tof.shape
    depth_rows = measured.shape[0]
    time_blocks = measured.shape[1] // width
    pixels = blocks * width
    sectors = lax.axis_size("sector")
    slabs = lax.axis_size("slab")
    groups = sectors // ZS
    terms = stops * blocks * slots
    rows = tof_rows.transpose(0, 2, 1)
    vmem = pl.BlockSpec(memory_space=pltpu.VMEM)
    smem = pl.BlockSpec(memory_space=pltpu.SMEM)
    f32, half, i32 = jnp.float32, jnp.bfloat16, jnp.int32
    field = (blocks, depth_rows, width)
    again = ITERS - 1
    ring = (groups, ZS, depth_rows // 4, width)
    results = pl.pallas_call(
        functools.partial(kernel, sectors, groups, slabs, blocks, time_blocks),
        out_shape=(
            jax.ShapeDtypeStruct((depth_rows, pixels), f32),
            jax.ShapeDtypeStruct(measured.shape, f32),
            jax.ShapeDtypeStruct((depth_rows, pixels), f32),
        ),
        in_specs=[smem, smem, vmem, vmem] + [pl.BlockSpec(memory_space=pl.ANY)] * 2,
        out_specs=(vmem, vmem, vmem),
        scratch_shapes=[
            pltpu.VMEM((stops, blocks, slots * width, width), half),
            pltpu.VMEM(measured.shape, f32),
            pltpu.VMEM((1, terms), i32),
            pltpu.VMEM((time_blocks, width), i32),
            pltpu.VMEM((sectors, width), i32),
            pltpu.SMEM((1, terms), i32),
            pltpu.SMEM((time_blocks, width), i32),
            pltpu.SMEM((sectors, width), i32),
            pltpu.VMEM((terms + 1, depth_rows, width), f32),
            pltpu.VMEM((time_blocks, depth_rows, width), half),
            pltpu.VMEM(field, f32),
            pltpu.VMEM(field, f32),
            pltpu.VMEM((blocks, width), f32),
            pltpu.VMEM(field, f32),
            pltpu.VMEM((again, stops) + field, half),
            pltpu.VMEM((ITERS, stops) + field, half),
            pltpu.VMEM((ITERS, stops) + field, half),
            pltpu.VMEM((2,) + field, f32),
            pltpu.VMEM((again, 2, blocks, width), f32),
            pltpu.VMEM((again, 2, blocks, width), f32),
            pltpu.VMEM((4 * blocks, depth_rows, width), f32),
            pltpu.VMEM((again,) + ring, f32),
            pltpu.VMEM((again, 2) + ring, f32),
            pltpu.VMEM((again,) + ring, f32),
            pltpu.VMEM(ring, f32),
            pltpu.VMEM((4, sectors, depth_rows // 4, width), f32),
            pltpu.VMEM((again,) + ring, f32),
            pltpu.VMEM((again,) + ring, f32),
            pltpu.SemaphoreType.DMA((stops + 1,)),
            pltpu.SemaphoreType.DMA((3,)),
            pltpu.SemaphoreType.DMA((again, stops)),
            pltpu.SemaphoreType.DMA((again, stops)),
            pltpu.SemaphoreType.DMA((ITERS, stops)),
            pltpu.SemaphoreType.DMA((ITERS, stops)),
            pltpu.SemaphoreType.DMA((again, 2)),
            pltpu.SemaphoreType.DMA((again, 2)),
            pltpu.SemaphoreType.DMA((again, 2, 2, ZS)),
            pltpu.SemaphoreType.DMA((again, 2, 2, ZS)),
        ],
        compiler_params=pltpu.CompilerParams(
            collective_id=0, has_side_effects=True, vmem_limit_bytes=60 * 1024 * 1024
        ),
    )(rows, tile_owner, rows, tile_owner[None], measured, tof.reshape(stops, blocks, slots * width, width))
    anywhere = pl.BlockSpec(memory_space=pl.ANY)
    return pl.pallas_call(
        deliver,
        out_shape=tuple(jax.ShapeDtypeStruct(r.shape, r.dtype) for r in results),
        in_specs=[anywhere] * 3,
        out_specs=(anywhere,) * 3,
        scratch_shapes=[pltpu.VMEM(r.shape, r.dtype) for r in results]
        + [pltpu.SemaphoreType.DMA((2, 3))],
    )(*results)


def solution(mesh):
    return jax.shard_map(
        body,
        mesh=mesh,
        in_specs=(
            P("slab", "sector"),
            P("sector", None, None, None, None),
            P("sector", None, None),
            P(),
        ),
        out_specs=(P("slab", "sector"), P("slab", "sector"), P("slab", "sector")),
        check_vma=False,
    )
```

```python
import functools

import jax
import jax.numpy as jnp
from jax import lax
from jax.experimental import pallas as pl
from jax.experimental.pallas import tpu as pltpu
from jax.sharding import PartitionSpec as P

ITERS = 3
STOPS = 8
HALF = STOPS // 2
ZS = 8

dual_step = 0.5
primal_step = 0.15
wave_limit = 0.5
depth_limit = 0.5


MET = (4, 2, 6, 3, 5, 1, 7, 0)
SENT = (0, 1, 7, 3, 5, 2, 6, 4)
HOPS = {0: -2, 1: -1, 7: 1, 3: -1, 5: 1, 2: -2, 6: 2}
UNROLL = 16


def kernel(
    sectors, groups, slabs, blocks, time_blocks,
    rows_ref, owner_ref, rows_block, owner_block, measured_hbm, tof_hbm,
    image_ref, data_ref, wave_ref,
    tof, measured_ref, prev_block, last_block, inverse_block, prev_ref, last_ref, inverse_ref, sums, dual_half, xbar, depth, halo, total,
    shares, part_out, part_in, relay, edge_out, edge_in,
    rolled, bands, turned, zed_out, zed_in, group_out, group_in, wave, rolled_back,
    load_sem, index_sem, share_send, share_recv, part_send, part_recv, edge_send, edge_recv,
    band_send, band_recv,
):
    me = lax.axis_index("sector")
    slab = lax.axis_index("slab")
    group, zed = me // ZS, lax.rem(me, ZS)
    terms = STOPS * blocks * 2

    loads = [
        pltpu.make_async_copy(tof_hbm.at[j], tof.at[j], load_sem.at[j]) for j in range(STOPS)
    ]
    measured_load = pltpu.make_async_copy(measured_hbm, measured_ref, load_sem.at[STOPS])
    measured_load.start()
    for j in SENT[:3]:
        loads[j].start()

    def sector_at(offset):
        return lax.rem(me + offset + sectors, sectors)

    def group_at(offset):
        return lax.rem(group + offset, groups)

    def zed_at(offset):
        return lax.rem(zed + offset, ZS)

    def slab_at(offset):
        return lax.rem(slab + offset + slabs, slabs)

    barrier = pltpu.get_barrier_semaphore()
    greeted = 0
    for hop in (1, -1, 2, -2):
        pl.semaphore_signal(barrier, inc=1, device_id={"sector": sector_at(hop)})
        greeted += 1
    for offset in range(1, ZS):
        pl.semaphore_signal(barrier, inc=1, device_id={"sector": group * ZS + zed_at(offset)})
        greeted += 1
    for offset in range(1, groups):
        pl.semaphore_signal(barrier, inc=1, device_id={"sector": group_at(offset) * ZS + zed})
        greeted += 1
    for sign in (1, -1):
        pl.semaphore_signal(barrier, inc=1, device_id={"slab": slab_at(sign)})
        greeted += 1

    lanes = lax.broadcasted_iota(jnp.int32, (4, 128), 1)
    quarter = lanes // 32
    odd_lane = lax.rem(lax.broadcasted_iota(jnp.int32, (ZS, 4, 128), 2), 2) == 1
    row_ids = lax.broadcasted_iota(jnp.int32, (16, 128), 0)
    last_slab = slab == slabs - 1
    first_slab = slab == 0

    def share_copy(it, j):
        source = {3: HALF, 5: HALF, 2: HALF, 6: HALF, 1: 2, 0: 2, 7: 6}[j]
        return pltpu.make_async_remote_copy(
            src_ref=shares.at[it, source], dst_ref=shares.at[it, j],
            send_sem=share_send.at[it, j], recv_sem=share_recv.at[it, j],
            device_id={"sector": sector_at(source - j)},
        )

    def part_copy(it, j):
        return pltpu.make_async_remote_copy(
            src_ref=part_out.at[it, j], dst_ref=part_in.at[it, j],
            send_sem=part_send.at[it, j], recv_sem=part_recv.at[it, j],
            device_id={"sector": sector_at(HOPS[j])},
        )

    def edge_copy(it, way):
        return pltpu.make_async_remote_copy(
            src_ref=edge_out.at[it, way], dst_ref=edge_in.at[it, way],
            send_sem=edge_send.at[it, way], recv_sem=edge_recv.at[it, way],
            device_id={"slab": slab_at(1 if way else -1)},
        )

    def zed_copy(it, way, offset):
        return pltpu.make_async_remote_copy(
            src_ref=zed_out.at[it, way, zed_at(offset)], dst_ref=zed_in.at[it, way, zed],
            send_sem=band_send.at[it, way, 0, offset], recv_sem=band_recv.at[it, way, 0, offset],
            device_id={"sector": group * ZS + zed_at(offset)},
        )

    def zed_wait(it, way, offset):
        pltpu.make_async_remote_copy(
            src_ref=zed_out.at[it, way, zed_at(offset)], dst_ref=zed_in.at[it, way, zed_at(ZS - offset)],
            send_sem=band_send.at[it, way, 0, offset], recv_sem=band_recv.at[it, way, 0, offset],
            device_id={"sector": group * ZS + zed_at(offset)},
        ).wait_recv()

    def group_copy(it, way, offset):
        return pltpu.make_async_remote_copy(
            src_ref=group_out.at[it, way, group_at(offset)], dst_ref=group_in.at[it, way, group],
            send_sem=band_send.at[it, way, 1, offset], recv_sem=band_recv.at[it, way, 1, offset],
            device_id={"sector": group_at(offset) * ZS + zed},
        )

    def group_wait(it, way, offset):
        pltpu.make_async_remote_copy(
            src_ref=group_out.at[it, way, group_at(offset)],
            dst_ref=group_in.at[it, way, group_at(groups - offset)],
            send_sem=band_send.at[it, way, 1, offset], recv_sem=band_recv.at[it, way, 1, offset],
            device_id={"sector": group_at(offset) * ZS + zed},
        ).wait_recv()

    def joined(pieces):
        return jnp.concatenate(pieces, 0).astype(jnp.bfloat16)

    def first_hop(it, way):
        for z in range(ZS):
            for q in range(groups // 4):
                zed_out[it, way, z, q] = joined([bands[4 * q + i, z] for i in range(4)])
        for offset in range(1, ZS):
            zed_copy(it, way, offset).start()
        zed_in[it, way, pl.ds(zed, 1)] = zed_out[it, way, pl.ds(zed, 1)]

    def second_hop(it, way):
        for offset in range(1, ZS):
            zed_wait(it, way, offset)
        for z in range(ZS):
            for q in range(groups // 4):
                value = zed_in[it, way, z, q].astype(jnp.float32)
                for i in range(4):
                    turned[4 * q + i, z] = value[4 * i : 4 * i + 4]
        for g in range(groups):
            for q in range(ZS // 4):
                group_out[it, way, g, q] = joined([turned[g, 4 * q + i] for i in range(4)])
        for offset in range(1, groups):
            group_copy(it, way, offset).start()
        group_in[it, way, pl.ds(group, 1)] = group_out[it, way, pl.ds(group, 1)]

    def finish_hops(it, way):
        for offset in range(1, groups):
            group_wait(it, way, offset)
        for g in range(groups):
            for q in range(ZS // 4):
                value = group_in[it, way, g, q].astype(jnp.float32)
                for i in range(4):
                    bands[g, 4 * q + i] = value[4 * i : 4 * i + 4]

    def forward_block(it, j, b, place):
        out = lax.dot_general(
            shares[it, j, b], tof[j, b], (((1,), (1,)), ((), ())),
            preferred_element_type=jnp.float32,
        )
        sums[place] = out[:, :128] + sums[prev_ref[0, place]]
        sums[place + blocks] = out[:, 128:]

    def adjoint_block(j, b):
        picked = jnp.concatenate([dual_half[rows_ref[j, 0, b]], dual_half[rows_ref[j, 1, b]]], 1)
        return jnp.dot(picked, tof[j, b], preferred_element_type=jnp.float32)

    sums[terms] = jnp.zeros((16, 128), jnp.float32)
    measured_load.wait()

    for t in range(time_blocks):
        span = slice(t * 128, (t + 1) * 128)
        dual = (dual_step * (0.0 - measured_ref[:, span])) / (1.0 + dual_step)
        data_ref[:, span] = dual
        dual_half[t] = dual.astype(jnp.bfloat16)

    for j in SENT[3:]:
        loads[j].start()
    pl.semaphore_wait(barrier, greeted)

    def each_block(work):
        def some(i, carry):
            for k in range(UNROLL):
                work(i * UNROLL + k)
            return carry

        lax.fori_loop(0, blocks // UNROLL, some, 0)

    def adjoint_stop(it, j, first):
        if first:
            loads[j].wait()

        def work(b):
            value = adjoint_block(j, b)
            if j == HALF:
                total[b] = value
            elif j in (2, 6):
                relay[j // 4, b] = value
            else:
                part_out[it, j, b] = value.astype(jnp.bfloat16)

        each_block(work)
        if j not in (HALF, 2, 6):
            part_copy(it, j).start()

    def adjoint_relay(it, j):
        arrivals = (0, 1) if j == 2 else (7,)
        for k in arrivals:
            part_copy(it, k).wait_recv()
        for b in range(blocks):
            value = relay[j // 4, b]
            for k in arrivals:
                value = value + part_in[it, k, b].astype(jnp.float32)
            part_out[it, j, b] = value.astype(jnp.bfloat16)
        part_copy(it, j).start()

    def back_block(it, b):
        value = total[b]
        for j in (3, 5, 6, 2):
            value = value + part_in[it, j, b].astype(jnp.float32)
        return value

    def arrived(it):
        for j in (3, 5, 6, 2):
            part_copy(it, j).wait_recv()

    def forward_stop(it, j):
        start = MET.index(j) * 2 * blocks
        each_block(lambda b: forward_block(it, j, b, start + b))
        for place in range(start + blocks, start + 2 * blocks):
            sums[place] = sums[place] + sums[prev_ref[0, place]]

    index_copies = [
        pltpu.make_async_copy(prev_block, prev_ref, index_sem.at[0]),
        pltpu.make_async_copy(last_block, last_ref, index_sem.at[1]),
        pltpu.make_async_copy(inverse_block, inverse_ref, index_sem.at[2]),
    ]

    def index_terms():
        flat = jnp.concatenate([rows_block[j, k : k + 1, :] for j in MET for k in range(2)], 1)
        shape = (time_blocks, terms)
        same = flat == lax.broadcasted_iota(jnp.int32, shape, 0)
        place = lax.broadcasted_iota(jnp.int32, shape, 1)
        seen = jnp.where(same, place, -1)
        span = 1
        while span < terms:
            moved = jnp.where(place >= span, pltpu.roll(seen, span, 1), -1)
            seen = jnp.maximum(seen, moved)
            span *= 2
        before = jnp.where(place >= 1, pltpu.roll(seen, 1, 1), -1)
        prev = jnp.max(jnp.where(same, before, -1), 0, keepdims=True)
        prev_block[...] = jnp.where(prev < 0, terms, prev)
        last = jnp.max(seen, 1, keepdims=True)
        last_block[...] = jnp.broadcast_to(jnp.where(last < 0, terms, last), last_block.shape)
        shape = (sectors, sectors)
        owned = owner_block[...] == lax.broadcasted_iota(jnp.int32, shape, 0)
        inverse = jnp.max(
            jnp.where(owned, lax.broadcasted_iota(jnp.int32, shape, 1), 0), 1, keepdims=True
        )
        inverse_block[...] = jnp.broadcast_to(inverse, inverse_block.shape)
        for copy in index_copies:
            copy.start()

    def publish(it):
        for b in range(blocks):
            shares[it, HALF, b] = xbar[b].astype(jnp.bfloat16)
        for j in (2, 6, 3, 5):
            share_copy(it, j).start()
        for b in range(blocks):
            edge_out[it, 0, pl.ds(b, 1)] = xbar[b, 0:1]
            edge_out[it, 1, pl.ds(b, 1)] = xbar[b, 15:16]
        edge_copy(it, 0).start()
        edge_copy(it, 1).start()
        for b in range(blocks):
            value = xbar[b]
            rolled[b] = value
            for a in range(1, 4):
                rolled[a * blocks + b] = pltpu.roll(value, 32 * a, 1)

        def gather_band(k, carry):
            j = inverse_ref[k, 0]
            block, lane = j // 4, lax.rem(j, 4)
            parts = [
                rolled[lax.rem(r - lane + 4, 4) * blocks + block, 4 * r : 4 * r + 4]
                for r in range(4)
            ]
            low = jnp.where(quarter == 0, parts[0], parts[1])
            high = jnp.where(quarter == 2, parts[2], parts[3])
            bands[k // ZS, lax.rem(k, ZS)] = jnp.where(quarter < 2, low, high)
            return carry

        lax.fori_loop(0, sectors, gather_band, 0, unroll=8)
        first_hop(it, 0)

    def haar(upper, lower):
        def pairs(value):
            right = pltpu.roll(value, 127, 2)
            left = pltpu.roll(value, 1, 2)
            return jnp.where(odd_lane, left - value, value + right)

        top, low = pairs(upper), pairs(lower)
        return (top + low) * 0.5, (top - low) * 0.5

    def update_wave(it):
        for g in range(groups):
            full = bands[g]
            upper = jnp.concatenate([full[2 * (i // 2)][None] for i in range(ZS)], 0)
            lower = jnp.concatenate([full[2 * (i // 2) + 1][None] for i in range(ZS)], 0)
            odd = lax.rem(lax.broadcasted_iota(jnp.int32, (ZS, 4, 128), 0), 2) == 1
            top, low = haar(upper, lower)
            coeffs = jnp.where(odd, low, top)
            kept = wave[g] + dual_step * coeffs
            dual = jnp.clip(kept, -wave_limit, wave_limit)
            wave[g] = dual
            upper = jnp.concatenate([dual[2 * (i // 2)][None] for i in range(ZS)], 0)
            lower = jnp.concatenate([dual[2 * (i // 2) + 1][None] for i in range(ZS)], 0)
            top, low = haar(upper, lower)
            bands[g] = jnp.where(odd, low, top)

    def update_depth(it):
        edge_copy(it, 0).wait_recv()
        edge_copy(it, 1).wait_recv()
        following = edge_in[it, 0]
        previous = edge_in[it, 1]
        for b in range(blocks):
            value = xbar[b]
            up = jnp.where(row_ids == 15, following[b : b + 1], pltpu.roll(value, 15, 0))
            diff = up - value
            diff = jnp.where(jnp.logical_and(last_slab, row_ids == 15), 0.0, diff)
            depth[b] = jnp.clip(depth[b] + dual_step * diff, -depth_limit, depth_limit)
        edge = halo[...] + dual_step * (edge_out[it, 0] - previous)
        edge = jnp.clip(edge, -depth_limit, depth_limit)
        halo[...] = jnp.where(first_slab, 0.0, edge)

    def spread_bands(source, count):
        for g in range(count // ZS):
            value = source(g)
            rolled_back[0, pl.ds(g * ZS, ZS)] = value
            for a in range(1, 4):
                rolled_back[a, pl.ds(g * ZS, ZS)] = pltpu.roll(value, 32 * a, 2)

    def joined_bands(index, b):
        places = [index(4 * b + q) for q in range(4)]
        out = []
        for r in range(4):
            parts = [rolled_back[(q - r) % 4, places[q]] for q in range(4)]
            low = jnp.where(quarter == 0, parts[0], parts[1])
            high = jnp.where(quarter == 2, parts[2], parts[3])
            out.append(jnp.where(quarter < 2, low, high))
        return out

    for j in SENT:
        adjoint_stop(0, j, True)
    index_terms()
    adjoint_relay(0, 6)
    adjoint_relay(0, 2)
    for copy in index_copies:
        copy.wait()
    arrived(0)
    for b in range(blocks):
        image = jnp.maximum(0.0 - primal_step * back_block(0, b), 0.0)
        image_ref[:, b * 128 : (b + 1) * 128] = image
        xbar[b] = 2.0 * image
        depth[b] = jnp.zeros((16, 128), jnp.float32)
    halo[...] = jnp.zeros_like(halo)
    wave[...] = jnp.zeros_like(wave)

    def iteration(it, carry):
        publish(it)
        forward_stop(it, HALF)
        share_copy(it, 2).wait_recv()
        share_copy(it, 0).start()
        share_copy(it, 1).start()
        share_copy(it, 6).wait_recv()
        share_copy(it, 7).start()
        second_hop(it, 0)
        forward_stop(it, 2)
        forward_stop(it, 6)
        for j in (3, 5):
            share_copy(it, j).wait_recv()
            forward_stop(it, j)
        finish_hops(it, 0)
        update_wave(it)
        first_hop(it, 1)
        update_depth(it)
        for j in (1, 7, 0):
            share_copy(it, j).wait_recv()
            forward_stop(it, j)
        for t in range(time_blocks):
            span = slice(t * 128, (t + 1) * 128)
            moved = sums[last_ref[t, 0]] - measured_ref[:, span]
            dual = (data_ref[:, span] + dual_step * moved) / (1.0 + dual_step)
            data_ref[:, span] = dual
            dual_half[t] = dual.astype(jnp.bfloat16)
        for j in SENT:
            adjoint_stop(it + 1, j, False)
        second_hop(it, 1)
        adjoint_relay(it + 1, 6)
        adjoint_relay(it + 1, 2)
        spread_bands(lambda g: wave[g], sectors)
        for b in range(blocks):
            for r, part in enumerate(joined_bands(lambda j: j, b)):
                wave_ref[4 * r : 4 * r + 4, b * 128 : (b + 1) * 128] = part
        finish_hops(it, 1)
        spread_bands(lambda g: bands[g], sectors)
        for b in range(blocks):
            for r, part in enumerate(joined_bands(lambda j: owner_ref[j], b)):
                total[b, 4 * r : 4 * r + 4] = total[b, 4 * r : 4 * r + 4] + part
        arrived(it + 1)
        for b in range(blocks):
            span = slice(b * 128, (b + 1) * 128)
            shifted = jnp.where(row_ids == 0, halo[b : b + 1], pltpu.roll(depth[b], 1, 0))
            update = back_block(it + 1, b) + (shifted - depth[b])
            old = image_ref[:, span]
            image = jnp.maximum(old - primal_step * update, 0.0)
            xbar[b] = 2.0 * image - old
            image_ref[:, span] = image
        return carry

    lax.fori_loop(0, ITERS - 1, iteration, 0)

    for j in range(STOPS):
        if j != HALF:
            for it in range(ITERS - 1):
                share_copy(it, j).wait_send()
            for it in range(ITERS):
                part_copy(it, j).wait_send()
    for it in range(ITERS - 1):
        edge_copy(it, 0).wait_send()
        edge_copy(it, 1).wait_send()
        for way in range(2):
            for offset in range(1, ZS):
                zed_copy(it, way, offset).wait_send()
            for offset in range(1, groups):
                group_copy(it, way, offset).wait_send()


def deliver(a, b, c, a_out, b_out, c_out, a_held, b_held, c_held, sem):
    ways = ((a, a_held, a_out), (b, b_held, b_out), (c, c_held, c_out))
    loads = [pltpu.make_async_copy(w[0], w[1], sem.at[0, i]) for i, w in enumerate(ways)]
    stores = [pltpu.make_async_copy(w[1], w[2], sem.at[1, i]) for i, w in enumerate(ways)]
    for load in loads:
        load.start()
    for load, store in zip(loads, stores):
        load.wait()
        store.start()
    for store in stores:
        store.wait()


def body(measured, tof, tof_rows, tile_owner):
    stops, blocks, slots, width, _ = tof.shape
    depth_rows = measured.shape[0]
    time_blocks = measured.shape[1] // width
    pixels = blocks * width
    sectors = lax.axis_size("sector")
    slabs = lax.axis_size("slab")
    groups = sectors // ZS
    terms = stops * blocks * slots
    rows = tof_rows.transpose(0, 2, 1)
    vmem = pl.BlockSpec(memory_space=pltpu.VMEM)
    smem = pl.BlockSpec(memory_space=pltpu.SMEM)
    f32, half, i32 = jnp.float32, jnp.bfloat16, jnp.int32
    field = (blocks, depth_rows, width)
    again = ITERS - 1
    ring = (groups, ZS, depth_rows // 4, width)
    results = pl.pallas_call(
        functools.partial(kernel, sectors, groups, slabs, blocks, time_blocks),
        out_shape=(
            jax.ShapeDtypeStruct((depth_rows, pixels), f32),
            jax.ShapeDtypeStruct(measured.shape, f32),
            jax.ShapeDtypeStruct((depth_rows, pixels), f32),
        ),
        in_specs=[smem, smem, vmem, vmem] + [pl.BlockSpec(memory_space=pl.ANY)] * 2,
        out_specs=(vmem, vmem, vmem),
        scratch_shapes=[
            pltpu.VMEM((stops, blocks, slots * width, width), half),
            pltpu.VMEM(measured.shape, f32),
            pltpu.VMEM((1, terms), i32),
            pltpu.VMEM((time_blocks, width), i32),
            pltpu.VMEM((sectors, width), i32),
            pltpu.SMEM((1, terms), i32),
            pltpu.SMEM((time_blocks, width), i32),
            pltpu.SMEM((sectors, width), i32),
            pltpu.VMEM((terms + 1, depth_rows, width), f32),
            pltpu.VMEM((time_blocks, depth_rows, width), half),
            pltpu.VMEM(field, f32),
            pltpu.VMEM(field, f32),
            pltpu.VMEM((blocks, width), f32),
            pltpu.VMEM(field, f32),
            pltpu.VMEM((again, stops) + field, half),
            pltpu.VMEM((ITERS, stops) + field, half),
            pltpu.VMEM((ITERS, stops) + field, half),
            pltpu.VMEM((2,) + field, f32),
            pltpu.VMEM((again, 2, blocks, width), f32),
            pltpu.VMEM((again, 2, blocks, width), f32),
            pltpu.VMEM((4 * blocks, depth_rows, width), f32),
            pltpu.VMEM(ring, f32),
            pltpu.VMEM(ring, f32),
            pltpu.VMEM((again, 2, ZS, groups // 4, 16, width), half),
            pltpu.VMEM((again, 2, ZS, groups // 4, 16, width), half),
            pltpu.VMEM((again, 2, groups, ZS // 4, 16, width), half),
            pltpu.VMEM((again, 2, groups, ZS // 4, 16, width), half),
            pltpu.VMEM(ring, f32),
            pltpu.VMEM((4, sectors, depth_rows // 4, width), f32),
            pltpu.SemaphoreType.DMA((stops + 1,)),
            pltpu.SemaphoreType.DMA((3,)),
            pltpu.SemaphoreType.DMA((again, stops)),
            pltpu.SemaphoreType.DMA((again, stops)),
            pltpu.SemaphoreType.DMA((ITERS, stops)),
            pltpu.SemaphoreType.DMA((ITERS, stops)),
            pltpu.SemaphoreType.DMA((again, 2)),
            pltpu.SemaphoreType.DMA((again, 2)),
            pltpu.SemaphoreType.DMA((again, 2, 2, ZS)),
            pltpu.SemaphoreType.DMA((again, 2, 2, ZS)),
        ],
        compiler_params=pltpu.CompilerParams(
            collective_id=0, has_side_effects=True, vmem_limit_bytes=60 * 1024 * 1024
        ),
    )(rows, tile_owner, rows, tile_owner[None], measured, tof.reshape(stops, blocks, slots * width, width))
    anywhere = pl.BlockSpec(memory_space=pl.ANY)
    return pl.pallas_call(
        deliver,
        out_shape=tuple(jax.ShapeDtypeStruct(r.shape, r.dtype) for r in results),
        in_specs=[anywhere] * 3,
        out_specs=(anywhere,) * 3,
        scratch_shapes=[pltpu.VMEM(r.shape, r.dtype) for r in results]
        + [pltpu.SemaphoreType.DMA((2, 3))],
    )(*results)


def solution(mesh):
    return jax.shard_map(
        body,
        mesh=mesh,
        in_specs=(
            P("slab", "sector"),
            P("sector", None, None, None, None),
            P("sector", None, None),
            P(),
        ),
        out_specs=(P("slab", "sector"), P("slab", "sector"), P("slab", "sector")),
        check_vma=False,
    )
```

```python
import functools

import jax
import jax.numpy as jnp
from jax import lax
from jax.experimental import pallas as pl
from jax.experimental.pallas import tpu as pltpu
from jax.sharding import PartitionSpec as P

ITERS = 3
STOPS = 8
HALF = STOPS // 2
ZS = 8

dual_step = 0.5
primal_step = 0.15
wave_limit = 0.5
depth_limit = 0.5


MET = (4, 2, 6, 3, 5, 1, 7, 0)
SENT = (0, 1, 7, 3, 5, 2, 6, 4)
HOPS = {0: -2, 1: -1, 7: 1, 3: -1, 5: 1, 2: -2, 6: 2}
UNROLL = 16


def kernel(
    sectors, groups, slabs, blocks, time_blocks,
    rows_ref, owner_ref, rows_block, owner_block, measured_hbm, tof_hbm,
    image_ref, data_ref, wave_ref,
    tof, measured_ref, prev_block, last_block, inverse_block, prev_ref, last_ref, inverse_ref, sums, dual_half, xbar, depth, halo, total,
    shares, part_out, part_in, relay, edge_out, edge_in,
    rolled, bands, turned, zed_out, zed_in, group_out, group_in, wave, rolled_back,
    load_sem, index_sem, share_send, share_recv, part_send, part_recv, edge_send, edge_recv,
    band_send, band_recv,
):
    me = lax.axis_index("sector")
    slab = lax.axis_index("slab")
    group, zed = me // ZS, lax.rem(me, ZS)
    terms = STOPS * blocks * 2

    loads = [
        pltpu.make_async_copy(tof_hbm.at[j], tof.at[j], load_sem.at[j]) for j in range(STOPS)
    ]
    measured_load = pltpu.make_async_copy(measured_hbm, measured_ref, load_sem.at[STOPS])
    measured_load.start()
    for j in SENT[:3]:
        loads[j].start()

    def sector_at(offset):
        return lax.rem(me + offset + sectors, sectors)

    def group_at(offset):
        return lax.rem(group + offset, groups)

    def zed_at(offset):
        return lax.rem(zed + offset, ZS)

    def slab_at(offset):
        return lax.rem(slab + offset + slabs, slabs)

    barrier = pltpu.get_barrier_semaphore()
    greeted = 0
    for hop in (1, -1, 2, -2):
        pl.semaphore_signal(barrier, inc=1, device_id={"sector": sector_at(hop)})
        greeted += 1
    for offset in range(1, ZS):
        pl.semaphore_signal(barrier, inc=1, device_id={"sector": group * ZS + zed_at(offset)})
        greeted += 1
    for offset in range(1, groups):
        pl.semaphore_signal(barrier, inc=1, device_id={"sector": group_at(offset) * ZS + zed})
        greeted += 1
    for sign in (1, -1):
        pl.semaphore_signal(barrier, inc=1, device_id={"slab": slab_at(sign)})
        greeted += 1

    lanes = lax.broadcasted_iota(jnp.int32, (4, 128), 1)
    quarter = lanes // 32
    odd_lane = lax.rem(lax.broadcasted_iota(jnp.int32, (ZS, 4, 128), 2), 2) == 1
    row_ids = lax.broadcasted_iota(jnp.int32, (16, 128), 0)
    last_slab = slab == slabs - 1
    first_slab = slab == 0

    def share_copy(it, j):
        source = {3: HALF, 5: HALF, 2: HALF, 6: HALF, 1: 2, 0: 2, 7: 6}[j]
        return pltpu.make_async_remote_copy(
            src_ref=shares.at[it, source], dst_ref=shares.at[it, j],
            send_sem=share_send.at[it, j], recv_sem=share_recv.at[it, j],
            device_id={"sector": sector_at(source - j)},
        )

    def part_copy(it, j):
        return pltpu.make_async_remote_copy(
            src_ref=part_out.at[it, j], dst_ref=part_in.at[it, j],
            send_sem=part_send.at[it, j], recv_sem=part_recv.at[it, j],
            device_id={"sector": sector_at(HOPS[j])},
        )

    def edge_copy(it, way):
        return pltpu.make_async_remote_copy(
            src_ref=edge_out.at[it, way], dst_ref=edge_in.at[it, way],
            send_sem=edge_send.at[it, way], recv_sem=edge_recv.at[it, way],
            device_id={"slab": slab_at(1 if way else -1)},
        )

    def zed_copy(it, way, offset):
        return pltpu.make_async_remote_copy(
            src_ref=zed_out.at[it, way, zed_at(offset)], dst_ref=zed_in.at[it, way, zed],
            send_sem=band_send.at[it, way, 0, offset], recv_sem=band_recv.at[it, way, 0, offset],
            device_id={"sector": group * ZS + zed_at(offset)},
        )

    def zed_wait(it, way, offset):
        pltpu.make_async_remote_copy(
            src_ref=zed_out.at[it, way, zed_at(offset)], dst_ref=zed_in.at[it, way, zed_at(ZS - offset)],
            send_sem=band_send.at[it, way, 0, offset], recv_sem=band_recv.at[it, way, 0, offset],
            device_id={"sector": group * ZS + zed_at(offset)},
        ).wait_recv()

    def group_copy(it, way, offset):
        return pltpu.make_async_remote_copy(
            src_ref=group_out.at[it, way, group_at(offset)], dst_ref=group_in.at[it, way, group],
            send_sem=band_send.at[it, way, 1, offset], recv_sem=band_recv.at[it, way, 1, offset],
            device_id={"sector": group_at(offset) * ZS + zed},
        )

    def group_wait(it, way, offset):
        pltpu.make_async_remote_copy(
            src_ref=group_out.at[it, way, group_at(offset)],
            dst_ref=group_in.at[it, way, group_at(groups - offset)],
            send_sem=band_send.at[it, way, 1, offset], recv_sem=band_recv.at[it, way, 1, offset],
            device_id={"sector": group_at(offset) * ZS + zed},
        ).wait_recv()

    def joined(pieces):
        return jnp.concatenate(pieces, 0).astype(jnp.bfloat16)

    def first_hop(it, way):
        for z in range(ZS):
            for q in range(groups // 4):
                zed_out[it, way, z, q] = joined([bands[4 * q + i, z] for i in range(4)])
        for offset in range(1, ZS):
            zed_copy(it, way, offset).start()
        zed_in[it, way, pl.ds(zed, 1)] = zed_out[it, way, pl.ds(zed, 1)]

    def second_hop(it, way):
        for offset in range(1, ZS):
            zed_wait(it, way, offset)
        for z in range(ZS):
            for q in range(groups // 4):
                value = zed_in[it, way, z, q].astype(jnp.float32)
                for i in range(4):
                    turned[4 * q + i, z] = value[4 * i : 4 * i + 4]
        for g in range(groups):
            for q in range(ZS // 4):
                group_out[it, way, g, q] = joined([turned[g, 4 * q + i] for i in range(4)])
        for offset in range(1, groups):
            group_copy(it, way, offset).start()
        group_in[it, way, pl.ds(group, 1)] = group_out[it, way, pl.ds(group, 1)]

    def finish_hops(it, way):
        for offset in range(1, groups):
            group_wait(it, way, offset)
        for g in range(groups):
            for q in range(ZS // 4):
                value = group_in[it, way, g, q].astype(jnp.float32)
                for i in range(4):
                    bands[g, 4 * q + i] = value[4 * i : 4 * i + 4]

    def forward_block(it, j, b, place):
        out = lax.dot_general(
            shares[it, j, b], tof[j, b], (((1,), (1,)), ((), ())),
            preferred_element_type=jnp.float32,
        )
        sums[place] = out[:, :128] + sums[prev_ref[0, place]]
        sums[place + blocks] = out[:, 128:]

    def adjoint_block(j, b):
        picked = jnp.concatenate([dual_half[rows_ref[j, 0, b]], dual_half[rows_ref[j, 1, b]]], 1)
        return jnp.dot(picked, tof[j, b], preferred_element_type=jnp.float32)

    sums[terms] = jnp.zeros((16, 128), jnp.float32)
    measured_load.wait()

    for t in range(time_blocks):
        span = slice(t * 128, (t + 1) * 128)
        dual = (dual_step * (0.0 - measured_ref[:, span])) / (1.0 + dual_step)
        data_ref[:, span] = dual
        dual_half[t] = dual.astype(jnp.bfloat16)

    for j in SENT[3:]:
        loads[j].start()
    pl.semaphore_wait(barrier, greeted)

    def each_block(work):
        def some(i, carry):
            for k in range(UNROLL):
                work(i * UNROLL + k)
            return carry

        lax.fori_loop(0, blocks // UNROLL, some, 0)

    def adjoint_stop(it, j, first):
        if first:
            loads[j].wait()

        def work(b):
            value = adjoint_block(j, b)
            if j == HALF:
                total[b] = value
            elif j in (2, 6):
                relay[j // 4, b] = value
            else:
                part_out[it, j, b] = value.astype(jnp.bfloat16)

        each_block(work)
        if j not in (HALF, 2, 6):
            part_copy(it, j).start()

    def adjoint_relay(it, j):
        arrivals = (0, 1) if j == 2 else (7,)
        for k in arrivals:
            part_copy(it, k).wait_recv()
        for b in range(blocks):
            value = relay[j // 4, b]
            for k in arrivals:
                value = value + part_in[it, k, b].astype(jnp.float32)
            part_out[it, j, b] = value.astype(jnp.bfloat16)
        part_copy(it, j).start()

    def back_block(it, b):
        value = total[b]
        for j in (3, 5, 6, 2):
            value = value + part_in[it, j, b].astype(jnp.float32)
        return value

    def arrived(it):
        for j in (3, 5, 6, 2):
            part_copy(it, j).wait_recv()

    def forward_stop(it, j):
        start = MET.index(j) * 2 * blocks
        each_block(lambda b: forward_block(it, j, b, start + b))
        for place in range(start + blocks, start + 2 * blocks):
            sums[place] = sums[place] + sums[prev_ref[0, place]]

    index_copies = [
        pltpu.make_async_copy(prev_block, prev_ref, index_sem.at[0]),
        pltpu.make_async_copy(last_block, last_ref, index_sem.at[1]),
        pltpu.make_async_copy(inverse_block, inverse_ref, index_sem.at[2]),
    ]

    def index_terms():
        flat = jnp.concatenate([rows_block[j, k : k + 1, :] for j in MET for k in range(2)], 1)
        shape = (time_blocks, terms)
        same = flat == lax.broadcasted_iota(jnp.int32, shape, 0)
        place = lax.broadcasted_iota(jnp.int32, shape, 1)
        seen = jnp.where(same, place, -1)
        span = 1
        while span < terms:
            moved = jnp.where(place >= span, pltpu.roll(seen, span, 1), -1)
            seen = jnp.maximum(seen, moved)
            span *= 2
        before = jnp.where(place >= 1, pltpu.roll(seen, 1, 1), -1)
        prev = jnp.max(jnp.where(same, before, -1), 0, keepdims=True)
        prev_block[...] = jnp.where(prev < 0, terms, prev)
        last = jnp.max(seen, 1, keepdims=True)
        last_block[...] = jnp.broadcast_to(jnp.where(last < 0, terms, last), last_block.shape)
        shape = (sectors, sectors)
        owned = owner_block[...] == lax.broadcasted_iota(jnp.int32, shape, 0)
        inverse = jnp.max(
            jnp.where(owned, lax.broadcasted_iota(jnp.int32, shape, 1), 0), 1, keepdims=True
        )
        inverse_block[...] = jnp.broadcast_to(inverse, inverse_block.shape)
        for copy in index_copies:
            copy.start()

    def publish(it):
        for b in range(blocks):
            shares[it, HALF, b] = xbar[b].astype(jnp.bfloat16)
        for j in (2, 6, 3, 5):
            share_copy(it, j).start()
        for b in range(blocks):
            edge_out[it, 0, pl.ds(b, 1)] = xbar[b, 0:1]
            edge_out[it, 1, pl.ds(b, 1)] = xbar[b, 15:16]
        edge_copy(it, 0).start()
        edge_copy(it, 1).start()
        for b in range(blocks):
            value = xbar[b]
            rolled[b] = value
            for a in range(1, 4):
                rolled[a * blocks + b] = pltpu.roll(value, 32 * a, 1)

        def gather_band(k, carry):
            j = inverse_ref[k, 0]
            block, lane = j // 4, lax.rem(j, 4)
            parts = [
                rolled[lax.rem(r - lane + 4, 4) * blocks + block, 4 * r : 4 * r + 4]
                for r in range(4)
            ]
            low = jnp.where(quarter == 0, parts[0], parts[1])
            high = jnp.where(quarter == 2, parts[2], parts[3])
            bands[k // ZS, lax.rem(k, ZS)] = jnp.where(quarter < 2, low, high)
            return carry

        lax.fori_loop(0, sectors, gather_band, 0, unroll=8)
        first_hop(it, 0)

    def haar(upper, lower):
        def pairs(value):
            right = pltpu.roll(value, 127, 2)
            left = pltpu.roll(value, 1, 2)
            return jnp.where(odd_lane, left - value, value + right)

        top, low = pairs(upper), pairs(lower)
        return (top + low) * 0.5, (top - low) * 0.5

    def update_wave(it):
        for g in range(groups):
            full = bands[g]
            upper = jnp.concatenate([full[2 * (i // 2)][None] for i in range(ZS)], 0)
            lower = jnp.concatenate([full[2 * (i // 2) + 1][None] for i in range(ZS)], 0)
            odd = lax.rem(lax.broadcasted_iota(jnp.int32, (ZS, 4, 128), 0), 2) == 1
            top, low = haar(upper, lower)
            coeffs = jnp.where(odd, low, top)
            kept = wave[g] + dual_step * coeffs
            dual = jnp.clip(kept, -wave_limit, wave_limit)
            wave[g] = dual
            upper = jnp.concatenate([dual[2 * (i // 2)][None] for i in range(ZS)], 0)
            lower = jnp.concatenate([dual[2 * (i // 2) + 1][None] for i in range(ZS)], 0)
            top, low = haar(upper, lower)
            bands[g] = jnp.where(odd, low, top)

    def update_depth(it):
        edge_copy(it, 0).wait_recv()
        edge_copy(it, 1).wait_recv()
        following = edge_in[it, 0]
        previous = edge_in[it, 1]
        for b in range(blocks):
            value = xbar[b]
            up = jnp.where(row_ids == 15, following[b : b + 1], pltpu.roll(value, 15, 0))
            diff = up - value
            diff = jnp.where(jnp.logical_and(last_slab, row_ids == 15), 0.0, diff)
            depth[b] = jnp.clip(depth[b] + dual_step * diff, -depth_limit, depth_limit)
        edge = halo[...] + dual_step * (edge_out[it, 0] - previous)
        edge = jnp.clip(edge, -depth_limit, depth_limit)
        halo[...] = jnp.where(first_slab, 0.0, edge)

    def spread_bands(source, count):
        for g in range(count // ZS):
            value = source(g)
            rolled_back[0, pl.ds(g * ZS, ZS)] = value
            for a in range(1, 4):
                rolled_back[a, pl.ds(g * ZS, ZS)] = pltpu.roll(value, 32 * a, 2)

    def joined_bands(index, b):
        places = [index(4 * b + q) for q in range(4)]
        out = []
        for r in range(4):
            parts = [rolled_back[(q - r) % 4, places[q]] for q in range(4)]
            low = jnp.where(quarter == 0, parts[0], parts[1])
            high = jnp.where(quarter == 2, parts[2], parts[3])
            out.append(jnp.where(quarter < 2, low, high))
        return out

    for j in SENT:
        adjoint_stop(0, j, True)
    index_terms()
    adjoint_relay(0, 6)
    adjoint_relay(0, 2)
    for copy in index_copies:
        copy.wait()
    arrived(0)
    for b in range(blocks):
        image = jnp.maximum(0.0 - primal_step * back_block(0, b), 0.0)
        image_ref[:, b * 128 : (b + 1) * 128] = image
        xbar[b] = 2.0 * image
        depth[b] = jnp.zeros((16, 128), jnp.float32)
    halo[...] = jnp.zeros_like(halo)
    wave[...] = jnp.zeros_like(wave)

    def iteration(it, carry):
        publish(it)
        forward_stop(it, HALF)
        share_copy(it, 2).wait_recv()
        share_copy(it, 0).start()
        share_copy(it, 1).start()
        share_copy(it, 6).wait_recv()
        share_copy(it, 7).start()
        second_hop(it, 0)
        forward_stop(it, 2)
        forward_stop(it, 6)
        for j in (3, 5):
            share_copy(it, j).wait_recv()
            forward_stop(it, j)
        share_copy(it, 1).wait_recv()
        forward_stop(it, 1)
        finish_hops(it, 0)
        update_wave(it)
        first_hop(it, 1)
        update_depth(it)
        for j in (7, 0):
            share_copy(it, j).wait_recv()
            forward_stop(it, j)
        for t in range(time_blocks):
            span = slice(t * 128, (t + 1) * 128)
            moved = sums[last_ref[t, 0]] - measured_ref[:, span]
            dual = (data_ref[:, span] + dual_step * moved) / (1.0 + dual_step)
            data_ref[:, span] = dual
            dual_half[t] = dual.astype(jnp.bfloat16)
        for j in SENT:
            adjoint_stop(it + 1, j, False)
        second_hop(it, 1)
        adjoint_relay(it + 1, 6)
        adjoint_relay(it + 1, 2)
        spread_bands(lambda g: wave[g], sectors)
        for b in range(blocks):
            for r, part in enumerate(joined_bands(lambda j: j, b)):
                wave_ref[4 * r : 4 * r + 4, b * 128 : (b + 1) * 128] = part
        finish_hops(it, 1)
        spread_bands(lambda g: bands[g], sectors)
        for b in range(blocks):
            for r, part in enumerate(joined_bands(lambda j: owner_ref[j], b)):
                total[b, 4 * r : 4 * r + 4] = total[b, 4 * r : 4 * r + 4] + part
        arrived(it + 1)
        for b in range(blocks):
            span = slice(b * 128, (b + 1) * 128)
            shifted = jnp.where(row_ids == 0, halo[b : b + 1], pltpu.roll(depth[b], 1, 0))
            update = back_block(it + 1, b) + (shifted - depth[b])
            old = image_ref[:, span]
            image = jnp.maximum(old - primal_step * update, 0.0)
            xbar[b] = 2.0 * image - old
            image_ref[:, span] = image
        return carry

    lax.fori_loop(0, ITERS - 1, iteration, 0)

    for j in range(STOPS):
        if j != HALF:
            for it in range(ITERS - 1):
                share_copy(it, j).wait_send()
            for it in range(ITERS):
                part_copy(it, j).wait_send()
    for it in range(ITERS - 1):
        edge_copy(it, 0).wait_send()
        edge_copy(it, 1).wait_send()
        for way in range(2):
            for offset in range(1, ZS):
                zed_copy(it, way, offset).wait_send()
            for offset in range(1, groups):
                group_copy(it, way, offset).wait_send()


def deliver(a, b, c, a_out, b_out, c_out, a_held, b_held, c_held, sem):
    ways = ((a, a_held, a_out), (b, b_held, b_out), (c, c_held, c_out))
    loads = [pltpu.make_async_copy(w[0], w[1], sem.at[0, i]) for i, w in enumerate(ways)]
    stores = [pltpu.make_async_copy(w[1], w[2], sem.at[1, i]) for i, w in enumerate(ways)]
    for load in loads:
        load.start()
    for load, store in zip(loads, stores):
        load.wait()
        store.start()
    for store in stores:
        store.wait()


def body(measured, tof, tof_rows, tile_owner):
    stops, blocks, slots, width, _ = tof.shape
    depth_rows = measured.shape[0]
    time_blocks = measured.shape[1] // width
    pixels = blocks * width
    sectors = lax.axis_size("sector")
    slabs = lax.axis_size("slab")
    groups = sectors // ZS
    terms = stops * blocks * slots
    rows = tof_rows.transpose(0, 2, 1)
    vmem = pl.BlockSpec(memory_space=pltpu.VMEM)
    smem = pl.BlockSpec(memory_space=pltpu.SMEM)
    f32, half, i32 = jnp.float32, jnp.bfloat16, jnp.int32
    field = (blocks, depth_rows, width)
    again = ITERS - 1
    ring = (groups, ZS, depth_rows // 4, width)
    results = pl.pallas_call(
        functools.partial(kernel, sectors, groups, slabs, blocks, time_blocks),
        out_shape=(
            jax.ShapeDtypeStruct((depth_rows, pixels), f32),
            jax.ShapeDtypeStruct(measured.shape, f32),
            jax.ShapeDtypeStruct((depth_rows, pixels), f32),
        ),
        in_specs=[smem, smem, vmem, vmem] + [pl.BlockSpec(memory_space=pl.ANY)] * 2,
        out_specs=(vmem, vmem, vmem),
        scratch_shapes=[
            pltpu.VMEM((stops, blocks, slots * width, width), half),
            pltpu.VMEM(measured.shape, f32),
            pltpu.VMEM((1, terms), i32),
            pltpu.VMEM((time_blocks, width), i32),
            pltpu.VMEM((sectors, width), i32),
            pltpu.SMEM((1, terms), i32),
            pltpu.SMEM((time_blocks, width), i32),
            pltpu.SMEM((sectors, width), i32),
            pltpu.VMEM((terms + 1, depth_rows, width), f32),
            pltpu.VMEM((time_blocks, depth_rows, width), half),
            pltpu.VMEM(field, f32),
            pltpu.VMEM(field, f32),
            pltpu.VMEM((blocks, width), f32),
            pltpu.VMEM(field, f32),
            pltpu.VMEM((again, stops) + field, half),
            pltpu.VMEM((ITERS, stops) + field, half),
            pltpu.VMEM((ITERS, stops) + field, half),
            pltpu.VMEM((2,) + field, f32),
            pltpu.VMEM((again, 2, blocks, width), f32),
            pltpu.VMEM((again, 2, blocks, width), f32),
            pltpu.VMEM((4 * blocks, depth_rows, width), f32),
            pltpu.VMEM(ring, f32),
            pltpu.VMEM(ring, f32),
            pltpu.VMEM((again, 2, ZS, groups // 4, 16, width), half),
            pltpu.VMEM((again, 2, ZS, groups // 4, 16, width), half),
            pltpu.VMEM((again, 2, groups, ZS // 4, 16, width), half),
            pltpu.VMEM((again, 2, groups, ZS // 4, 16, width), half),
            pltpu.VMEM(ring, f32),
            pltpu.VMEM((4, sectors, depth_rows // 4, width), f32),
            pltpu.SemaphoreType.DMA((stops + 1,)),
            pltpu.SemaphoreType.DMA((3,)),
            pltpu.SemaphoreType.DMA((again, stops)),
            pltpu.SemaphoreType.DMA((again, stops)),
            pltpu.SemaphoreType.DMA((ITERS, stops)),
            pltpu.SemaphoreType.DMA((ITERS, stops)),
            pltpu.SemaphoreType.DMA((again, 2)),
            pltpu.SemaphoreType.DMA((again, 2)),
            pltpu.SemaphoreType.DMA((again, 2, 2, ZS)),
            pltpu.SemaphoreType.DMA((again, 2, 2, ZS)),
        ],
        compiler_params=pltpu.CompilerParams(
            collective_id=0, has_side_effects=True, vmem_limit_bytes=60 * 1024 * 1024
        ),
    )(rows, tile_owner, rows, tile_owner[None], measured, tof.reshape(stops, blocks, slots * width, width))
    anywhere = pl.BlockSpec(memory_space=pl.ANY)
    return pl.pallas_call(
        deliver,
        out_shape=tuple(jax.ShapeDtypeStruct(r.shape, r.dtype) for r in results),
        in_specs=[anywhere] * 3,
        out_specs=(anywhere,) * 3,
        scratch_shapes=[pltpu.VMEM(r.shape, r.dtype) for r in results]
        + [pltpu.SemaphoreType.DMA((2, 3))],
    )(*results)


def solution(mesh):
    return jax.shard_map(
        body,
        mesh=mesh,
        in_specs=(
            P("slab", "sector"),
            P("sector", None, None, None, None),
            P("sector", None, None),
            P(),
        ),
        out_specs=(P("slab", "sector"), P("slab", "sector"), P("slab", "sector")),
        check_vma=False,
    )
```
